512 devices in a mesh: inner: 16 (over x_lo, z), outer: 32 (over x_hi, y, core).
Axes of the slice: x: 4 (x_hi: 2, x_lo: 2; x = x_hi * 2 + x_lo), y: 8, z: 8, core: 2. Of those that a mesh axis runs over, the one named last changes fastest.
Arguments:
- queries: float32 [65536, 1024], P(('outer', 'inner')), may hold values from -150 to 150, as said below
- keys: float32 [65536, 128], P(('outer', 'inner')), may hold values from -5 to 5
- values: float32 [65536, 128], P(('outer', 'inner')), may hold values from -6 to 6
- segment: int32 [65536], P(('outer', 'inner')), may hold values from 0 to 255, never falling along the last dimension, each value on 1 to 2048 neighbouring positions
Outputs:
- attended: float32 [65536, 1024], P(('outer', 'inner'))
The draws below stay inside these ranges and needn't reach their ends.
Inputs may be any that keep to these rules, and one draw needn't show every extreme that they name: queries of a few tokens may be large multiples of earlier keys. `segment`: a trajectory holds at most 2048 tokens.
All inputs are finite; a program needn't handle non-finite values.
Results may differ from the reference program's by a relative error of at most 0.0003.
Values sent between devices are 32-bit elements; how exact they have to be, the bound alone decides.
A program may use at most 64 MiB of HBM per device.

```python
import math
import jax
import jax.numpy as jnp
import numpy as np
from jax import lax

HEAD_DIM = 128
HEADS = 8
TOK_DEV = 128
GROUP = 2048
SEQ = 65536
SEGS = 256


def drawn_rows(key):
    base = jnp.clip(jax.random.normal(jax.random.fold_in(key, 11), (SEQ, HEAD_DIM), jnp.float32), -5.0, 5.0)
    return base


def draw_keys(key, part):
    base = drawn_rows(key)
    return base


def draw_queries(key, part):
    key = jax.random.fold_in(key, 2)
    drawn = jnp.clip(jax.random.normal(key, (SEQ, HEADS * HEAD_DIM), jnp.float32), -5.0, 5.0)
    return drawn


def level_of(stream_key, extent, shards, smallest, top_value):
    level, own = 1.0, jax.random.fold_in(stream_key, 6)
    for dim, blocks in shards:
        heights = jnp.exp(jax.random.uniform(jax.random.fold_in(own, dim), (blocks,), jnp.float32, smallest / len(shards), top_value / len(shards)))
        level = level * jnp.repeat(heights, extent[dim] // blocks).reshape([-1 if axis == dim else 1 for axis in range(len(extent))])
    return level


def split_up(count, total, bound, lean):
    loads = [(1 << 20) // math.isqrt(grade ** lean) + 1 for grade in range(2, count + 1)]
    spare, counts = total - bound - (count - 1), [1] * (count - 1)
    while spare > 0:
        free = [i for i in range(count - 1) if counts[i] < bound]
        whole, budget = sum([loads[i] for i in free]), spare
        for i in free:
            more = min(bound - counts[i], max(1, budget * loads[i] // whole), spare)
            counts[i] = counts[i] + more
            spare = spare - more
    return np.array([bound] + counts)


def uneven_parts(stream_key, number_of, total, most, skew):
    if number_of == 2:
        one = jax.random.randint(stream_key, (), max(1, total - most), min(most, total - 1) + 1)
        return jnp.stack([one, total - one])
    sizes = jnp.asarray(split_up(number_of, total, most, skew), jnp.int32)
    pairs = (number_of - 1) // 2
    source_of, taker = sizes[1:1 + 2 * pairs:2], sizes[2:2 + 2 * pairs:2]
    slack = jnp.minimum(source_of - 1, most - taker)
    shifted = jax.random.randint(jax.random.fold_in(stream_key, 1), (pairs,), 0, 1 << 20) % (slack + 1)
    sizes = sizes.at[1:1 + 2 * pairs:2].set(source_of - shifted).at[2:2 + 2 * pairs:2].set(taker + shifted)
    return sizes[jax.random.permutation(jax.random.fold_in(stream_key, 2), number_of)]


def normal_values(rng, shape, deviation, bound, split=(), kind=jnp.bfloat16):
    result = jax.random.normal(rng, shape, jnp.float32) * deviation
    if len(split) > 0:
        result = level_of(rng, shape, split, -0.22, 0.18) * result
    return jnp.clip(result, min=-bound, max=bound).astype(kind)


def setup_inputs(seed: int = 0) -> dict:
    splits = jax.random.split(jax.random.key(seed), 5)
    return {
        "queries": draw_queries(jax.random.fold_in(splits[4], 71), 0),
        "keys": draw_keys(jax.random.fold_in(splits[4], 71), 0),
        "values": normal_values(splits[2], (SEQ, HEAD_DIM), 1.0, 6.0, ((0, 512),), jnp.float32),
        "segment": jnp.searchsorted(jnp.cumsum(uneven_parts(splits[3], SEGS, SEQ, GROUP, 2)), jnp.arange(SEQ), side="right").astype(jnp.int32),
    }


def reference(queries, keys, values, segment):
    scale = 1.0 / (HEAD_DIM ** 0.5)
    pad_keys = jnp.concatenate([jnp.zeros((GROUP, HEAD_DIM), jnp.float32), keys], axis=0)
    pad_values = jnp.concatenate([jnp.zeros((GROUP, HEAD_DIM), jnp.float32), values], axis=0)
    pad_segment = jnp.concatenate([jnp.full((GROUP,), -1, jnp.int32), segment.astype(jnp.int32)], axis=0)
    window = GROUP + TOK_DEV

    def one_block(block):
        first = (block * TOK_DEV).astype(jnp.int32)
        query_rows = lax.dynamic_slice(queries, (first, jnp.int32(0)), (TOK_DEV, HEADS * HEAD_DIM))
        query_rows = query_rows.reshape(TOK_DEV, HEADS, HEAD_DIM)
        key_rows = lax.dynamic_slice(pad_keys, (first, jnp.int32(0)), (window, HEAD_DIM))
        value_rows = lax.dynamic_slice(pad_values, (first, jnp.int32(0)), (window, HEAD_DIM))
        key_segment = lax.dynamic_slice(pad_segment, (first,), (window,))
        query_segment = lax.dynamic_slice(segment.astype(jnp.int32), (first,), (TOK_DEV,))
        query_pos = first + jnp.arange(TOK_DEV, dtype=jnp.int32)
        key_pos = first - GROUP + jnp.arange(window, dtype=jnp.int32)
        visible = (key_segment[None, :] == query_segment[:, None]) & (key_pos[None, :] <= query_pos[:, None])
        scores = jnp.einsum("thd,kd->thk", query_rows, key_rows, precision=lax.Precision.HIGHEST) * scale
        scores = jnp.where(visible[:, None, :], scores, -1e30)
        top = jnp.max(scores, axis=-1, keepdims=True)
        weights = jnp.where(visible[:, None, :], jnp.exp(scores - top), 0.0)
        total = jnp.sum(weights, axis=-1)
        mixed = jnp.einsum("thk,kd->thd", weights, value_rows, precision=lax.Precision.HIGHEST)
        return (mixed / total[..., None]).reshape(TOK_DEV, HEADS * HEAD_DIM)

    blocks = lax.map(one_block, jnp.arange(SEQ // TOK_DEV, dtype=jnp.int32))
    return blocks.reshape(SEQ, HEADS * HEAD_DIM)
```

```python
import functools
import math

import jax
import jax.numpy as jnp
from jax import lax
from jax.experimental import pallas as pl
from jax.experimental.pallas import tpu as pltpu
from jax.sharding import PartitionSpec as P

MESH = pl.DeviceIdType.MESH
F32, BF16 = jnp.float32, jnp.bfloat16

TOK = 128
HEADS = 8
SLOTS = 16
RING = 8
KEY_ROWS = TOK + 8
ROWS = KEY_ROWS + TOK
PARTS = ((0, KEY_ROWS), (KEY_ROWS, TOK))
MASKED = -1e30

ROUTES = (
    (1138688, 32580615, 77625346, 78672899, 5271556, 344070),
    (326435840, 9754632, 10501442, 338704693, 11849741, 1032204),
    (93390096, 77619266, 78675011, 72382532, 12612678, 475143),
    (9897985, 8707120, 325069251, 14691343, 272643381, 835596),
    (94439697, 78712064, 12652569, 32576520, 74479686, 475149),
    (10947586, 272639025, 8437771, 15741239, 273692982, 835597),
    (95489298, 79761665, 13702170, 268507145, 14711879, 475144),
    (11997187, 273688626, 9487372, 326156301, 14695686, 835592),
    (96538899, 80811266, 14751771, 74776586, 15802625, 475145),
    (13046788, 274738227, 10536973, 50381838, 15737095, 835593),
    (97588500, 81860867, 74776604, 336608267, 76810312, 475146),
    (14096389, 275787828, 11586574, 8439823, 9486385, 835594),
    (98638101, 74776852, 336622671, 337670216, 77859913, 475147),
    (15145990, 15742005, 8400948, 52438067, 11584522, 835584),
    (91543872, 324338783, 337672264, 30483764, 29436227, 507979),
    (15367, 14688262, 13640709, 12587018, 2100235, 786433),
    (1056768, 15737863, 10487814, 11537413, 13643780, 868366),
    (872227848, 871180528, 869326017, 203479883, 204527420, 245812),
    (77357057, 77596672, 78646279, 5320710, 81793101, 999439),
    (253700105, 1019018296, 870516784, 869469239, 56373302, 49156),
    (78406658, 3147528, 4194379, 80747596, 5249102, 999503),
    (254749706, 52179001, 871424195, 870318084, 57422903, 49157),
    (79456259, 4197129, 5243980, 7419981, 6373128, 999424),
    (255799307, 53228602, 1107140, 871424005, 6348558, 49152),
    (80505860, 5246730, 6293581, 83697742, 8135680, 999425),
    (256848908, 54278203, 2156741, 58778630, 7537423, 49153),
    (81555461, 6296331, 7343182, 81736, 815793993, 999426),
    (257898509, 55327804, 3206342, 59776058, 202432704, 49154),
    (82605062, 6103836, 4275207, 1049417, 816843594, 999427),
    (258948110, 208720957, 201379900, 202434619, 8587321, 49155),
    (871178247, 870130783, 882907136, 868226049, 5057538, 1032195),
    (8641551, 56819726, 55772173, 54724620, 204482571, 9),
)


def split(x):
    high = x.astype(BF16)
    return high, (x - high.astype(F32)).astype(BF16)


def bits(word, low, count):
    return lax.rem(lax.div(word, jnp.int32(1 << low)), jnp.int32(1 << count))


def doubled(x):
    high, low = split(x)
    return jnp.concatenate(
        [jnp.concatenate([high, high], axis=1), jnp.concatenate([low, low], axis=1)], axis=0
    )


def attend(kv, slot, mask, first, q_ref, acc, top, total):
    keys = doubled(kv[slot, 0:TOK, :])
    values = doubled(kv[slot, KEY_ROWS:ROWS, :].T)
    mask = jnp.concatenate([mask, mask], axis=1)
    for pair in range(HEADS // 2):
        cols = slice(pair * 2 * TOK, (pair + 1) * 2 * TOK)
        both = jnp.dot(keys, q_ref[:, cols], preferred_element_type=F32)
        scores = jnp.where(mask, both[:TOK] + both[TOK:], MASKED)
        high = jnp.max(scores, axis=0, keepdims=True)
        if not first:
            old = top[0:1, cols]
            high = jnp.maximum(old, high)
            factor = jnp.exp2(old - high)
        weights = jnp.exp2(scores - high)
        added = jnp.sum(weights, axis=0, keepdims=True)
        both = jnp.dot(values, jnp.concatenate(split(weights), axis=0), preferred_element_type=F32)
        mixed = both[:TOK] + both[TOK:]
        top[0:1, cols] = high
        if first:
            total[0:1, cols] = added
            acc[:, cols] = mixed
        else:
            total[0:1, cols] = total[0:1, cols] * factor + added
            acc[:, cols] = acc[:, cols] * factor + mixed


def kernel(
    planes, queries, keys, values, segment, out, kv, q_raw, q_ref, acc, top, total,
    load_sem, send_sem, extra_sem, recv_sem,
):
    inner, outer = lax.axis_index("inner"), lax.axis_index("outer")
    x, z = lax.div(inner, RING), lax.rem(inner, RING)
    plane, core = lax.div(outer, 2), lax.rem(outer, 2)
    up, down, across = lax.rem(z + 1, RING), lax.rem(z + RING - 1, RING), 1 - x
    ahead, behind = lax.rem(plane + 1, planes), lax.rem(plane + planes - 1, planes)

    def at(to_plane, to_x, to_z, to_core):
        return {"inner": to_x * RING + to_z, "outer": to_plane * 2 + to_core}

    near = [(x, up), (x, down), (across, z)]
    barrier = pltpu.get_barrier_semaphore()

    def greet(device):
        pl.semaphore_signal(barrier, inc=1, device_id=device, device_id_type=MESH)

    for to_x, to_z in near:
        for to_core in (0, 1):
            greet(at(plane, to_x, to_z, to_core))
    greet(at(plane, x, z, 1 - core))

    @pl.when(core == 0)
    def _():
        greet(at(behind, x, z, 1))

    @pl.when((core == 0) & (x == 0))
    def _():
        greet(at(behind, 1, z, 1))

    own = SLOTS
    loads = [
        pltpu.make_async_copy(keys, kv.at[own, pl.ds(0, TOK)], load_sem.at[0]),
        pltpu.make_async_copy(values, kv.at[own, pl.ds(KEY_ROWS, TOK)], load_sem.at[1]),
        pltpu.make_async_copy(queries, q_raw, load_sem.at[2]),
    ]
    for load in loads:
        load.start()
    own_seg = segment[...].astype(F32)
    kv[own, TOK:KEY_ROWS, :] = jnp.broadcast_to(own_seg, (8, TOK))

    place = inner * 2 + core
    words = [jnp.int32(0)] * 6
    for row, packed in enumerate(ROUTES):
        words = [jnp.where(place == row, jnp.int32(p), w) for p, w in zip(packed, words)]

    def entry(step):
        third, rest = lax.div(step, 3), lax.rem(step, 3)
        word = words[0]
        for n in range(1, 6):
            word = jnp.where(third == n, words[n], word)
        word = jnp.where(
            rest == 0, word, jnp.where(rest == 1, lax.div(word, 1 << 10), lax.div(word, 1 << 20))
        )
        return lax.rem(word, 1 << 10)

    def piece(held, slot, part, device, sem):
        first, count = PARTS[part]
        return pltpu.make_async_remote_copy(
            src_ref=kv.at[held, pl.ds(first, count)],
            dst_ref=kv.at[slot, pl.ds(first, count)],
            send_sem=sem,
            recv_sem=recv_sem.at[slot, part],
            device_id=device,
            device_id_type=MESH,
        )

    def onward(route, held, slot, part, act):
        for way, (to_x, to_z) in enumerate(near):
            device = at(plane, to_x, to_z, bits(route, 5 + 2 * way, 1))

            @pl.when(bits(route, 4 + 2 * way, 1) == 1)
            def _():
                act(piece(held, slot, part, device, send_sem.at[way, held, part]))

    def own_extra(part, act):
        @pl.when(core == 0)
        def _():
            act(piece(own, inner, part, at(plane, x, z, 1), extra_sem.at[0, part]))

        @pl.when(core == 1)
        def _():
            act(piece(own, inner, part, at(ahead, x, z, 0), extra_sem.at[0, part]))

        @pl.when((core == 1) & (x == 1))
        def _():
            act(piece(own, inner, part, at(ahead, 0, z, 0), extra_sem.at[1, part]))

    def start(copy):
        copy.start()

    def finish(copy):
        copy.wait_send()

    own_route = entry(jnp.int32(SLOTS))
    pl.semaphore_wait(barrier, 7 + core * (1 + x))
    loads[0].wait()
    onward(own_route, own, inner, 0, start)
    own_extra(0, start)
    loads[1].wait()
    onward(own_route, own, inner, 1, start)
    own_extra(1, start)

    loads[2].wait()
    scale = math.log2(math.e) / math.sqrt(TOK)
    for head in range(HEADS):
        cols = slice(head * TOK, (head + 1) * TOK)
        q_high, q_low = split(q_raw[:, cols].T * scale)
        q_ref[0:TOK, cols] = q_high
        q_ref[TOK : 2 * TOK, cols] = q_low

    row = lax.broadcasted_iota(jnp.int32, (TOK, TOK), 0)
    col = lax.broadcasted_iota(jnp.int32, (TOK, TOK), 1)
    seg_all = jnp.broadcast_to(own_seg, (TOK, TOK))
    attend(kv, own, (seg_all.T == seg_all) & (row <= col), True, q_ref, acc, top, total)

    lead = own_seg[:, 0:1]

    def step(n, carry):
        route = entry(n)
        slot = bits(route, 0, 4)
        for part in (0, 1):
            piece(slot, slot, part, at(plane, x, up, core), send_sem.at[0, slot, part]).wait_recv()
            onward(route, slot, slot, part, start)
        seg = kv[slot, TOK : TOK + 1, :]
        shared = jnp.sum(jnp.where(seg == lead, 1.0, 0.0), axis=1, keepdims=True)
        begin = jnp.where(own_seg == lead, TOK - shared, float(TOK))
        attend(kv, slot, row.astype(F32) >= begin, False, q_ref, acc, top, total)
        return carry

    lax.fori_loop(0, SLOTS, step, 0)

    for head in range(HEADS):
        cols = slice(head * TOK, (head + 1) * TOK)
        out[:, cols] = (acc[:, cols] / total[0:1, cols]).T

    def drain(n, carry):
        route = entry(n)
        slot = bits(route, 0, 4)
        for part in (0, 1):
            onward(route, slot, slot, part, finish)
        return carry

    lax.fori_loop(0, SLOTS, drain, 0)
    for part in (0, 1):
        onward(own_route, own, inner, part, finish)
        own_extra(part, finish)


def body(queries, keys, values, segment):
    planes = lax.axis_size("outer") // 2
    return pl.pallas_call(
        functools.partial(kernel, planes),
        name="gather_and_attend",
        out_shape=jax.ShapeDtypeStruct(queries.shape, F32),
        in_specs=[pl.BlockSpec(memory_space=pl.ANY)] * 3 + [pl.BlockSpec(memory_space=pltpu.VMEM)],
        out_specs=pl.BlockSpec(memory_space=pltpu.VMEM),
        scratch_shapes=[
            pltpu.VMEM((SLOTS + 1, ROWS, TOK), F32),
            pltpu.VMEM((TOK, HEADS * TOK), F32),
            pltpu.VMEM((2 * TOK, HEADS * TOK), BF16),
            pltpu.VMEM((TOK, HEADS * TOK), F32),
            pltpu.VMEM((8, HEADS * TOK), F32),
            pltpu.VMEM((8, HEADS * TOK), F32),
            pltpu.SemaphoreType.DMA((3,)),
            pltpu.SemaphoreType.DMA((3, SLOTS + 1, 2)),
            pltpu.SemaphoreType.DMA((2, 2)),
            pltpu.SemaphoreType.DMA((SLOTS, 2)),
        ],
        compiler_params=pltpu.CompilerParams(
            collective_id=0, has_side_effects=True, vmem_limit_bytes=24 << 20
        ),
    )(queries, keys, values, segment.reshape(1, TOK))


def solution(mesh):
    return jax.shard_map(
        body,
        mesh=mesh,
        in_specs=(
            P(("outer", "inner"), None),
            P(("outer", "inner"), None),
            P(("outer", "inner"), None),
            P(("outer", "inner")),
        ),
        out_specs=P(("outer", "inner"), None),
        check_vma=False,
    )
```

```python
import functools
import math

import jax
import jax.numpy as jnp
from jax import lax
from jax.experimental import pallas as pl
from jax.experimental.pallas import tpu as pltpu
from jax.sharding import PartitionSpec as P

MESH = pl.DeviceIdType.MESH
F32, BF16 = jnp.float32, jnp.bfloat16

TOK = 128
HEADS = 8
RING = 8
SLOTS = 16
PASSING = SLOTS
OWN = SLOTS + RING
KEY_ROWS = TOK + 8
ROWS = KEY_ROWS + TOK
PARTS = ((0, KEY_ROWS), (KEY_ROWS, TOK))
UP_HOPS = (4, 3)
LAG = 12
MASKED = -1e30

PLAN = (
    (278710033, 696010752, 311828512, 924845751, 694591521, 7612418, 556834486, 312576143, 859028486, 70931494, 11680309, 558420003, 380811269, 4404261, 12619885, 44, 2589072, 12465914, 50389),
    (820993, 679217184, 712804424, 10098792, 711527465, 116407306, 676375331, 575679566, 45650030, 47199812, 12332, 0, 0, 0, 0, 0, 9990657, 15049718, 52555),
    (412124161, 925280018, 704645760, 825567266, 859462954, 728763528, 279977492, 860004387, 314202215, 150591492, 12827684, 40424454, 216314389, 47289390, 5133, 0, 3809425, 7293816, 24044),
    (9470977, 841066242, 808583178, 8552554, 79306531, 112726056, 16552615, 49296070, 576297004, 48829454, 13357, 0, 0, 0, 0, 0, 3187345, 13584312, 56918),
    (705694337, 825632866, 859220105, 671091945, 704679700, 314364235, 559569924, 594579592, 8181068, 13636908, 593534184, 382768662, 106961039, 14727215, 0, 0, 236065, 5737547, 61293),
    (135301122, 44270602, 842016515, 809512041, 843186283, 8617996, 46667399, 14455912, 543243815, 49911853, 14382, 0, 0, 0, 0, 0, 12139026, 7703556, 61293),
    (3836546, 894043171, 860521867, 71444907, 178398997, 244592676, 315228981, 560496709, 862033165, 315628055, 81827976, 42523655, 15768942, 47, 0, 0, 4895026, 7164105, 63464),
    (36703362, 876620962, 910296107, 810559649, 844116074, 43102217, 543293453, 8486957, 82321190, 115907624, 48143, 0, 0, 0, 0, 0, 10570531, 6347205, 65144),
    (37753475, 416110243, 449631874, 828446370, 282105473, 571617078, 246723590, 211851799, 863118606, 43301098, 604536839, 8469543, 41263, 0, 0, 0, 1387572, 10397373, 36720),
    (12619780, 46929027, 12424355, 14424258, 47417387, 202386214, 544253966, 9471086, 15771495, 67141679, 40968, 0, 0, 0, 0, 0, 2839492, 7465581, 33017),
    (38803076, 417159844, 450681475, 896539299, 283154572, 8183426, 316846592, 906010210, 146095617, 144944431, 111158817, 310420488, 0, 0, 0, 0, 12991813, 12519214, 35233),
    (13669381, 47978628, 13473956, 82582659, 846367788, 15740014, 49327298, 302090240, 8455178, 101721130, 42024, 0, 0, 0, 0, 0, 3957973, 195559, 38938),
    (829430405, 418092070, 805966647, 776386567, 214998816, 181681795, 538479983, 539853964, 180625417, 146311529, 10530152, 42, 0, 0, 0, 0, 7360086, 10228733, 43906),
    (812685318, 846337038, 13866030, 15990980, 49516589, 8466720, 46138499, 370183272, 9439243, 102802475, 43018, 0, 0, 0, 0, 0, 5070454, 1281039, 41627),
    (8127110, 906663975, 452597135, 907712321, 675554446, 277002754, 841328164, 310906061, 640857098, 46346538, 11307, 0, 0, 0, 0, 0, 1437799, 14166350, 48291),
    (15768583, 116654214, 269779110, 8524878, 173127969, 9516072, 47188100, 304124009, 3156044, 36808748, 44043, 0, 0, 0, 0, 0, 14747383, 2399621, 45996),
    (837393, 696010760, 42654752, 694159218, 2106401, 10493033, 36362771, 49323023, 44047219, 14683797, 48311334, 112776227, 38810629, 38359604, 46207021, 12, 7508352, 11789999, 50389),
    (270313225, 815833096, 370541199, 504146607, 615778958, 786729095, 684957483, 584194051, 372415020, 38934092, 4132, 0, 0, 0, 0, 0, 717193, 7175138, 17859),
    (34612225, 857843474, 679487490, 780183586, 695206675, 101501955, 37411851, 7884815, 4872299, 13422639, 37854774, 113252366, 559469614, 5280870, 46093, 0, 565905, 12877747, 54638),
    (403743753, 849839882, 816980226, 917741858, 134754959, 852147459, 686132448, 585243652, 373464621, 39983693, 5157, 0, 0, 0, 0, 0, 12069401, 8270031, 22228),
    (10488457, 44141225, 101713683, 11538227, 826941475, 4956203, 13422592, 33657495, 594588181, 5323783, 559953717, 40942629, 6871149, 48338958, 0, 0, 11737641, 16105544, 59095),
    (143697930, 817301673, 169248897, 272380779, 306032776, 273167592, 852624015, 168410404, 552122437, 41033061, 6182, 0, 0, 0, 0, 0, 13308570, 1002883, 26462),
    (3844746, 826942475, 45786211, 35719988, 827330572, 104902657, 861544481, 38810629, 47798888, 6839296, 81822518, 7355430, 41475182, 47, 0, 0, 12761402, 886036, 63462),
    (45100170, 473706666, 507293833, 137114793, 237110532, 373458733, 274217096, 308066408, 6423119, 375423535, 39943, 0, 0, 0, 0, 0, 2702507, 6194205, 30223),
    (12587659, 105666219, 861546540, 715133955, 828476429, 47850533, 861964354, 15311878, 107502593, 7439406, 40910647, 49914376, 32, 0, 0, 0, 5483595, 1993005, 3975),
    (145797132, 179704589, 145199917, 178526030, 307433262, 238566537, 136583209, 308479791, 7439522, 106504, 33063, 0, 0, 0, 0, 0, 15355324, 2554165, 1921),
    (13637260, 106715820, 862596141, 14686212, 783323927, 70301734, 681582391, 545295375, 2730023, 49283593, 100764520, 35169281, 0, 0, 0, 0, 7032156, 9414462, 6402),
    (146846733, 180754190, 146249518, 274862927, 239910059, 8530278, 137632810, 309339496, 203465891, 67143681, 294945, 0, 0, 0, 0, 0, 16473805, 3639908, 297),
    (14686861, 107656983, 683719479, 7345928, 784372751, 116432680, 682622980, 34088036, 915410539, 1084938, 2664545, 34, 0, 0, 0, 0, 9199213, 10159351, 10771),
    (821082126, 854988941, 147298541, 275911944, 240427180, 212870439, 112333097, 268603393, 137439521, 104103978, 34818, 0, 0, 0, 0, 0, 9203198, 1358197, 8970),
    (8135310, 847951887, 684768359, 795718, 848999462, 68162656, 39332492, 583012449, 38643714, 582060555, 35843, 0, 0, 0, 0, 0, 14088078, 11277577, 15140),
    (148945935, 182852872, 278371624, 311564493, 174392493, 268578826, 312837253, 302158956, 304098370, 104901764, 3107, 0, 0, 0, 0, 0, 14252271, 379414, 13490),
)


def split(x):
    high = x.astype(BF16)
    return high, (x - high.astype(F32)).astype(BF16)


def across_lanes(both, blocks):
    return [
        both[:, 2 * n * TOK : (2 * n + 1) * TOK] + both[:, (2 * n + 1) * TOK : 2 * (n + 1) * TOK]
        for n in range(blocks)
    ]


def attend(kv, slots, masks, first, q_ref, acc, top, total):
    keys, values = [], []
    for slot in slots:
        k_high, k_low = split(kv[slot, 0:TOK, :])
        keys += [jnp.concatenate([k_high, k_high], axis=1), jnp.concatenate([k_low, k_low], axis=1)]
        values.append(jnp.concatenate(split(kv[slot, KEY_ROWS:ROWS, :]), axis=1))
    keys, values = jnp.concatenate(keys, axis=0), jnp.concatenate(values, axis=0)
    both = lax.dot_general(
        q_ref[...], keys, (((1,), (1,)), ((), ())), preferred_element_type=F32
    )
    scores = [
        jnp.where(jnp.concatenate([mask] * HEADS, axis=0), score, MASKED)
        for mask, score in zip(masks, across_lanes(both, len(slots)))
    ]
    high = functools.reduce(jnp.maximum, scores)
    high = jnp.broadcast_to(jnp.max(high, axis=1, keepdims=True), high.shape)
    if not first:
        old = top[...]
        high = jnp.maximum(old, high)
        factor = jnp.exp2(old - high)
    top[...] = high
    weights = [jnp.exp2(score - high) for score in scores]
    added = functools.reduce(jnp.add, weights)
    w_high, w_low = zip(*[split(weight) for weight in weights])
    both = jnp.dot(jnp.concatenate(w_high, axis=1), values, preferred_element_type=F32)
    rest = jnp.dot(jnp.concatenate(w_low, axis=1), values[:, :TOK], preferred_element_type=F32)
    mixed = across_lanes(both, 1)[0] + rest
    total[...] = added if first else total[...] * factor + added
    acc[...] = mixed if first else acc[...] * factor + mixed


def kernel(
    planes, queries, keys, values, segment, out, kv, q_raw, q_ref, acc, top, total,
    load_sem, send_sem, recv_sem,
):
    inner, outer = lax.axis_index("inner"), lax.axis_index("outer")
    x, z = lax.div(inner, RING), lax.rem(inner, RING)
    plane, core = lax.div(outer, 2), lax.rem(outer, 2)
    up, down, across = lax.rem(z + 1, RING), lax.rem(z + RING - 1, RING), 1 - x
    ahead, behind = lax.rem(plane + 1, planes), lax.rem(plane + planes - 1, planes)

    def at(to_plane, to_x, to_z, to_core):
        return {"inner": to_x * RING + to_z, "outer": to_plane * 2 + to_core}

    barrier = pltpu.get_barrier_semaphore()

    def greet(device):
        pl.semaphore_signal(barrier, inc=1, device_id=device, device_id_type=MESH)

    for to_x, to_z in ((x, up), (x, down), (across, z)):
        for to_core in (0, 1):
            greet(at(plane, to_x, to_z, to_core))
    greet(at(plane, x, z, 1 - core))

    @pl.when(core == 0)
    def _():
        greet(at(behind, x, z, 0))
        greet(at(behind, x, z, 1))

    @pl.when((core == 0) & (x == 0))
    def _():
        greet(at(behind, 1, z, 1))

    loads = [
        pltpu.make_async_copy(keys, kv.at[OWN, pl.ds(0, TOK)], load_sem.at[0]),
        pltpu.make_async_copy(values, kv.at[OWN, pl.ds(KEY_ROWS, TOK)], load_sem.at[1]),
        pltpu.make_async_copy(queries, q_raw, load_sem.at[2]),
    ]
    for load in loads:
        load.start()
    own_seg = segment[...].astype(F32)
    kv[OWN, TOK:KEY_ROWS, :] = jnp.broadcast_to(own_seg, (8, TOK))

    place = inner * 2 + core
    words = [jnp.int32(0)] * 19
    for row, packed in enumerate(PLAN):
        words = [jnp.where(place == row, jnp.int32(p), w) for p, w in zip(packed, words)]

    def lookup(options, n, each, width):
        word, rest = lax.div(n, each), lax.rem(n, each)
        packed = options[0]
        for k in range(1, len(options)):
            packed = jnp.where(word == k, options[k], packed)
        field = lax.rem(packed, 1 << width)
        for k in range(1, each):
            field = jnp.where(
                rest == k, lax.rem(lax.div(packed, 1 << (width * k)), 1 << width), field
            )
        return field

    def event_of(n):
        return lookup(words[:16], n, 3, 10)

    def slot_of(n):
        return lookup(words[16:], n, 6, 4)

    def bit(event, place):
        return lax.rem(lax.div(event, 1 << place), 2) == 1

    def piece(held, slot, part, device, way):
        first, count = PARTS[part]
        return pltpu.make_async_remote_copy(
            src_ref=kv.at[held, pl.ds(first, count)],
            dst_ref=kv.at[slot, pl.ds(first, count)],
            send_sem=send_sem.at[way, held, part],
            recv_sem=recv_sem.at[slot, part],
            device_id=device,
            device_id_type=MESH,
        )


    def onward(event, part, act):
        held = lax.rem(event, 32)
        index, passing = lax.rem(held, RING), held >= PASSING
        crossed = (held < PASSING) & (lax.div(held, RING) != x)
        is_o = passing | (~crossed & (core == 1) & (index < z))
        here = x * RING + index
        for way, to_z in ((0, up), (1, down)):
            below = index < to_z
            to_core = jnp.where(crossed, core, jnp.where(is_o == below, 1, 0))
            to_slot = jnp.where(is_o, jnp.where(below, here, PASSING + index), held)

            @pl.when(bit(event, 7 + way))
            def _():
                act(piece(held, to_slot, part, at(plane, x, to_z, to_core), way))

        @pl.when(bit(event, 9))
        def _():
            aside = {
                "inner": jnp.where(is_o, inner, across * RING + z),
                "outer": jnp.where(is_o, ahead * 2, plane * 2 + x),
            }
            act(piece(held, here, part, aside, 2))

    def own_onward(part, act):
        for way, to_z in ((0, up), (1, down)):
            hops = lax.rem(to_z - z + RING, RING)
            below = z < to_z
            to_core = jnp.where((core == 1) == below, 1, 0)
            to_slot = jnp.where((core == 1) & ~below, PASSING + z, inner)
            act(piece(OWN, to_slot, part, at(plane, x, to_z, to_core), way))

        @pl.when(core == 0)
        def _():
            act(piece(OWN, inner, part, at(plane, across, z, x), 2))
            act(piece(OWN, inner, part, at(plane, x, z, 1), 3))

        @pl.when(core == 1)
        def _():
            act(piece(OWN, inner, part, at(ahead, x, z, 0), 3))
            crossing = {
                "inner": across * RING + z,
                "outer": jnp.where(x == 0, plane * 2 + 1, ahead * 2),
            }
            act(piece(OWN, inner, part, crossing, 2))

    def start(copy):
        copy.start()

    def finish(copy):
        copy.wait_send()

    pl.semaphore_wait(barrier, 8 + core * x)
    for part in (0, 1):
        loads[part].wait()
        own_onward(part, start)

    loads[2].wait()
    scale = math.log2(math.e) / math.sqrt(TOK)
    for head in range(HEADS):
        rows = slice(head * TOK, (head + 1) * TOK)
        q_high, q_low = split(q_raw[:, rows] * scale)
        q_ref[rows, 0:TOK] = q_high
        q_ref[rows, TOK : 2 * TOK] = q_low

    row = lax.broadcasted_iota(jnp.int32, (TOK, TOK), 0)
    col = lax.broadcasted_iota(jnp.int32, (TOK, TOK), 1)
    seg_row = jnp.broadcast_to(own_seg, (TOK, TOK))
    seg_col = seg_row.T
    attend(kv, [OWN], [(seg_col == seg_row) & (col <= row)], True, q_ref, acc, top, total)

    lead = own_seg[:, 0:1]
    pieces = 2 * (SLOTS + (1 - core) * (RING - 1 - z))

    def pair(n):
        slots = [slot_of(2 * n), slot_of(2 * n + 1)]
        masks = []
        for slot in slots:
            seg = kv[slot, TOK : TOK + 1, :]
            shared = jnp.sum(jnp.where(seg == lead, 1.0, 0.0), axis=1, keepdims=True)
            masks.append((seg_col == lead) & (col.astype(F32) >= TOK - shared))
        attend(kv, slots, masks, False, q_ref, acc, top, total)

    def each_part(event, do):
        for part in (0, 1):

            @pl.when(bit(event, 5) == (part == 1))
            def _():
                do(part)

    def step(n, paired):
        event = event_of(n)

        def receive(part):
            slot = lax.rem(event, 32)
            piece(slot, slot, part, at(plane, x, up, core), 0).wait_recv()
            onward(event, part, start)

        each_part(event, receive)
        now = bit(event, 6)

        @pl.when(now)
        def _():
            pair(paired)

        @pl.when(n >= LAG)
        def _():
            drain(n - LAG, 0)

        return paired + jnp.where(now, 1, 0)

    def drain(n, carry):
        event = event_of(n)

        @pl.when(event >= 1 << 7)
        def _():
            each_part(event, lambda part: onward(event, part, finish))

        return carry

    paired = lax.fori_loop(0, pieces, step, jnp.int32(0))

    def rest(n, carry):
        pair(n)
        return carry

    lax.fori_loop(paired, SLOTS // 2, rest, 0)

    for head in range(HEADS):
        rows = slice(head * TOK, (head + 1) * TOK)
        out[:, rows] = acc[rows, :] / jnp.sum(total[rows, :], axis=1, keepdims=True)

    lax.fori_loop(pieces - LAG, pieces, drain, 0)
    for part in (0, 1):
        own_onward(part, finish)


def body(queries, keys, values, segment):
    planes = lax.axis_size("outer") // 2
    rows = HEADS * TOK
    return pl.pallas_call(
        functools.partial(kernel, planes),
        name="gather_and_attend",
        out_shape=jax.ShapeDtypeStruct(queries.shape, F32),
        in_specs=[pl.BlockSpec(memory_space=pltpu.HBM)] * 3 + [pl.BlockSpec(memory_space=pltpu.VMEM)],
        out_specs=pl.BlockSpec(memory_space=pltpu.VMEM),
        scratch_shapes=[
            pltpu.VMEM((OWN + 1, ROWS, TOK), F32),
            pltpu.VMEM((TOK, rows), F32),
            pltpu.VMEM((rows, 2 * TOK), BF16),
            pltpu.VMEM((rows, TOK), F32),
            pltpu.VMEM((rows, TOK), F32),
            pltpu.VMEM((rows, TOK), F32),
            pltpu.SemaphoreType.DMA((3,)),
            pltpu.SemaphoreType.DMA((4, OWN + 1, 2)),
            pltpu.SemaphoreType.DMA((OWN, 2)),
        ],
        compiler_params=pltpu.CompilerParams(
            collective_id=0, has_side_effects=True, vmem_limit_bytes=60 << 20
        ),
    )(queries, keys, values, segment.reshape(1, TOK))


def solution(mesh):
    return jax.shard_map(
        body,
        mesh=mesh,
        in_specs=(
            P(("outer", "inner"), None),
            P(("outer", "inner"), None),
            P(("outer", "inner"), None),
            P(("outer", "inner")),
        ),
        out_specs=P(("outer", "inner"), None),
        check_vma=False,
    )
```

```python
import functools
import math

import jax
import jax.numpy as jnp
from jax import lax
from jax.experimental import pallas as pl
from jax.experimental.pallas import tpu as pltpu
from jax.sharding import PartitionSpec as P

MESH = pl.DeviceIdType.MESH
F32, BF16 = jnp.float32, jnp.bfloat16

TOK = 128
HEADS = 8
RING = 8
SLOTS = 16
PASSING = SLOTS
OWN = SLOTS + RING
KEY_ROWS = TOK + 8
ROWS = KEY_ROWS + TOK
PARTS = ((0, KEY_ROWS), (KEY_ROWS, TOK))
UP_HOPS = (4, 3)
LAG = 12
MASKED = -1e30

PLAN = (
    (278710033, 34359296, 695607593, 35440641, 69918120, 694164746, 149981715, 728016935, 183507827, 11538069, 592481382, 5388852, 182997355, 47395877, 71348260, 12, 7504272, 15415034, 50389),
    (820993, 679217248, 9150242, 9478790, 710977027, 111164490, 14728995, 575745669, 112758830, 47779853, 12332, 0, 0, 0, 0, 0, 9990657, 15070118, 52555),
    (412124161, 925280018, 704645760, 825329930, 143445290, 558521347, 103981323, 8180407, 71981355, 13162639, 183603239, 314579509, 39991893, 47233061, 13317, 0, 9052305, 13584307, 54758),
    (807437313, 908108809, 44171274, 8618755, 12357255, 712090116, 678203499, 49295439, 575713894, 48829454, 13357, 0, 0, 0, 0, 0, 3187345, 7293816, 56924),
    (2786945, 825632866, 859220105, 671091945, 704679700, 314364235, 143152132, 105536780, 314745653, 594555973, 316168199, 660749349, 49289255, 14727270, 0, 0, 236065, 6146123, 59127),
    (135301122, 11275489, 9546531, 11577092, 167881856, 8467236, 46800389, 578589800, 16259149, 49395238, 47118, 0, 0, 0, 0, 0, 12165906, 7703616, 61398),
    (3836546, 826379905, 860521867, 211201162, 5002410, 105132201, 382523008, 282072608, 316168293, 561830024, 109066246, 7920678, 40910190, 47, 0, 0, 10137906, 9261252, 63462),
    (36833283, 136057058, 168832804, 810559595, 9449578, 134329125, 543175721, 8434784, 41958246, 644921863, 48143, 0, 0, 0, 0, 0, 11211811, 7145925, 63464),
    (707793539, 673993764, 449631692, 672143010, 145790285, 383289110, 179448630, 144202758, 40085774, 537713705, 8461614, 82878048, 41263, 0, 0, 0, 1387587, 15297213, 36720),
    (137400324, 844336901, 113379340, 170661899, 135375885, 115120138, 14713898, 48244295, 43007847, 100711424, 40968, 0, 0, 0, 0, 0, 11715892, 8264406, 33017),
    (38803076, 895891108, 862369411, 7102179, 40503566, 8182924, 537112878, 838966818, 146030145, 179448111, 44115489, 310386793, 0, 0, 0, 0, 15088965, 12519212, 35233),
    (138449925, 845386502, 114428941, 170930951, 48279566, 78777127, 35695695, 77642752, 75792385, 42042410, 41993, 0, 0, 0, 0, 0, 12834373, 994174, 38938),
    (39852677, 418143909, 451731076, 75141888, 108822669, 249171215, 385388033, 147621378, 180659273, 310521160, 44050978, 43, 0, 0, 0, 0, 7360086, 13180733, 47656),
    (139499526, 846436103, 115478542, 15742208, 49329316, 137376096, 46138376, 11640867, 76548449, 45196322, 43018, 0, 0, 0, 0, 0, 13952854, 1588239, 43922),
    (8002304, 710975264, 452724175, 710706885, 675494153, 539272366, 148476168, 11307304, 248818179, 45298211, 11372, 0, 0, 0, 0, 0, 5371504, 10650782, 48189),
    (268475399, 241467526, 139723791, 303046767, 48403470, 13737986, 43066500, 38045741, 3223626, 113282090, 44043, 0, 0, 0, 0, 0, 5371399, 4381070, 48186),
    (837393, 34359304, 924885655, 10148865, 2139169, 7350934, 35667475, 858823722, 6340278, 11537422, 48976934, 37344299, 81317893, 624997413, 71348260, 12, 10654080, 3925751, 50389),
    (270313225, 815898632, 687210785, 720798506, 686065986, 719461963, 3317611, 305273549, 241743404, 139498060, 4133, 0, 0, 0, 0, 0, 15769993, 13859810, 17862),
    (34612225, 858605609, 11149314, 44736546, 859655168, 78646304, 45634199, 104520711, 694162228, 12622863, 593607716, 39890950, 558971445, 5346350, 46093, 0, 688785, 13584187, 54758),
    (403743753, 849839882, 371335426, 917676811, 687082624, 720536076, 686666083, 306322436, 175683182, 140547661, 5158, 0, 0, 0, 0, 0, 12069401, 14992368, 22231),
    (714082953, 44140554, 102517761, 11538227, 826314376, 696427, 13422596, 558927968, 695211116, 594550581, 40932365, 47765583, 49289750, 48248934, 0, 0, 11737641, 7717896, 59133),
    (44180490, 135505282, 236727714, 818155307, 851807368, 550768872, 687116416, 5473069, 551851631, 40050222, 6183, 0, 0, 0, 0, 0, 3871386, 15783052, 26597),
    (715132554, 37364747, 69250836, 714919970, 4272129, 46171925, 5345928, 578828149, 559939685, 33600518, 39861110, 594655767, 40909831, 47, 0, 0, 1649466, 874572, 63462),
    (144747531, 885172611, 918693283, 177475714, 306317069, 919766242, 551818376, 853841000, 552605888, 653295910, 39943, 0, 0, 0, 0, 0, 4834219, 15043858, 32518),
    (12587659, 681611947, 70300437, 37399349, 13633541, 35690326, 6956077, 81790774, 34642473, 7887982, 16327479, 116957287, 32768, 0, 0, 0, 5483595, 14772690, 3975),
    (145797132, 180106628, 212645348, 138164485, 853906602, 274932899, 308821122, 854721641, 7374050, 109051912, 33063, 0, 0, 0, 0, 0, 5952700, 3118654, 1921),
    (13637260, 828413612, 4861037, 81826614, 40545286, 681621507, 863080215, 545261575, 82877994, 827439, 33655305, 34670121, 0, 0, 0, 0, 7032156, 9402942, 6402),
    (146846733, 181156229, 146651557, 139214150, 921873702, 8530148, 44309635, 309497192, 43124809, 101746689, 294912, 0, 0, 0, 0, 0, 11986381, 7572047, 297),
    (14686861, 829528749, 863645742, 8134661, 4209765, 40943276, 682623784, 613449828, 915975171, 36767242, 102279170, 34, 0, 0, 0, 0, 16539245, 10159239, 8611),
    (147896334, 182205830, 214810022, 275911944, 240427180, 76688679, 112501892, 239371265, 137373952, 111185184, 2082, 0, 0, 0, 0, 0, 9238238, 4307317, 10800),
    (16399112, 847951879, 684825647, 6357769, 39945001, 547358381, 35336197, 849350757, 548407916, 581994532, 35907, 0, 0, 0, 0, 0, 622478, 13259222, 15140),
    (276872207, 310779022, 278371502, 311564493, 174306561, 214205450, 46273792, 173320480, 11831362, 37792900, 3171, 0, 0, 0, 0, 0, 14253711, 5901334, 13490),
    (278710033, 695510802, 729598344, 694591754, 556940353, 251320618, 693143347, 33565696, 313735733, 36229122, 148093460, 41006087, 70299660, 106990598, 37786629, 4, 129673, 13098539, 17763),
    (820993, 9242656, 840999559, 110110375, 15739526, 111843843, 842020911, 116003851, 575247403, 47779917, 12332, 0, 0, 0, 0, 0, 9906177, 12468134, 52549),
    (446450057, 1704754, 772024353, 2403091, 103599767, 729305224, 313696523, 71094934, 13162639, 659590319, 4740396, 7387342, 104870957, 6329447, 5158, 0, 8560665, 14599163, 22132),
    (9470977, 841812009, 111280138, 9178272, 42765959, 45784075, 843717188, 49295439, 642822758, 115872782, 46093, 0, 0, 0, 0, 0, 3187345, 7293816, 56924),
    (413828737, 178015369, 858786282, 103568000, 381321483, 558894900, 142881431, 594579253, 4366700, 105404429, 593640749, 38845445, 74463278, 6331494, 0, 0, 11545233, 16599235, 26597),
    (135301122, 111313930, 43001603, 809512803, 843164800, 12656800, 42606085, 911776812, 15808006, 49395238, 47118, 0, 0, 0, 0, 0, 11770386, 5752836, 61398),
    (672828034, 706096916, 145609131, 827329673, 281192681, 928026240, 382238724, 282613796, 862303767, 14819333, 316708407, 106961000, 7355439, 39, 0, 0, 3840786, 15062208, 32616),
    (36703362, 809512098, 843252779, 44270602, 79701765, 911254572, 543293453, 8500256, 912275975, 644921384, 48143, 0, 0, 0, 0, 0, 10570531, 7144860, 63464),
    (828018307, 861287042, 828813986, 672412676, 146060388, 179930934, 145316869, 863118606, 178295849, 570949998, 106970118, 74522927, 40999, 0, 0, 0, 1920035, 959899, 34806),
    (137400324, 46928908, 12358883, 45881474, 10717197, 203200557, 544290858, 34650121, 82880359, 100711424, 40968, 0, 0, 0, 0, 0, 2839492, 7465581, 33017),
    (829067908, 674674061, 830115702, 283772933, 39640204, 6851072, 40155372, 284755744, 179616971, 9995466, 111191047, 310483976, 0, 0, 0, 0, 12735444, 1831022, 34729),
    (138449925, 47200006, 13473956, 879769731, 48279715, 136392551, 45088783, 49293410, 111443969, 42042376, 41993, 0, 0, 0, 0, 0, 12805333, 994174, 38938),
    (830117509, 863637902, 776387328, 284171040, 181613606, 538643759, 839982627, 146810370, 572892199, 213131436, 10595624, 42, 0, 0, 0, 0, 14025957, 2715967, 43916),
    (14718982, 116137093, 14523557, 268450948, 116559917, 8749068, 46271489, 104105000, 2106443, 35761193, 43018, 0, 0, 0, 0, 0, 5076454, 3247119, 41657),
    (711721606, 452411168, 777782917, 148905761, 41554185, 378714690, 344754724, 10663053, 312844803, 45714572, 11308, 0, 0, 0, 0, 0, 7429894, 9249950, 48186),
    (140549127, 49298688, 8749222, 81925377, 173311016, 9450606, 69248132, 12619885, 3221794, 36808748, 44043, 0, 0, 0, 0, 0, 1574647, 2415077, 45996),
    (837393, 695239442, 729597960, 34643969, 2840585, 727819795, 36490247, 693148682, 39849030, 592460842, 36814388, 72896526, 48245797, 37752939, 46183501, 12, 7508352, 15024038, 52555),
    (270313225, 815898632, 687210785, 787907370, 371865858, 719461899, 3317611, 305273549, 174699053, 38934092, 4132, 0, 0, 0, 0, 0, 15769993, 13859810, 17862),
    (824214529, 679480114, 713139209, 75810, 858827539, 3824736, 36707860, 859872951, 12277764, 13162502, 39955492, 16274997, 5353509, 48348174, 46093, 0, 665745, 13022323, 57077),
    (403743753, 849839882, 371335426, 917676811, 687082624, 720536076, 753709411, 585243652, 584228196, 39983693, 5157, 0, 0, 0, 0, 0, 12069401, 5161968, 22231),
    (714082953, 1058914, 101755667, 679481139, 780947491, 859832324, 695238667, 12626980, 46208533, 595383303, 627088485, 14211078, 15840294, 49330190, 0, 0, 8591913, 7719744, 65238),
    (143697930, 135505282, 236727714, 142872363, 176459532, 201593708, 687116813, 654095584, 585644037, 41098533, 6182, 0, 0, 0, 0, 0, 3871386, 16581832, 26462),
    (3844746, 893423241, 859835049, 4195426, 12594965, 861544481, 578858020, 559944812, 6394944, 34396695, 7354381, 661697574, 15841319, 47, 0, 0, 4270394, 6315147, 65149),
    (144747531, 818285802, 918981769, 177475714, 306317069, 919766242, 274217096, 135051368, 6831461, 586520608, 39943, 0, 0, 0, 0, 0, 4834219, 6196498, 32608),
    (716182155, 13390948, 715132554, 5288757, 828377187, 6395529, 14473250, 561055273, 14791718, 8182817, 612408366, 33555048, 48143, 0, 0, 0, 5491275, 14800530, 61575),
    (145797132, 180106628, 820884964, 178525322, 307433262, 274959497, 43125263, 854787366, 7439522, 109051912, 33063, 0, 0, 0, 0, 0, 15389884, 3107125, 1921),
    (717231756, 682727190, 6296374, 14330916, 39861079, 863643693, 545826819, 103856135, 2137609, 102761320, 68190761, 34716687, 0, 0, 0, 0, 14070876, 2651114, 7945),
    (146846733, 180754190, 146249518, 888279302, 239376555, 8530799, 137632810, 309339432, 43124963, 101746753, 294912, 0, 0, 0, 0, 0, 7036621, 3640052, 297),
    (718281357, 82598950, 862983820, 7387912, 41594981, 70440, 33657483, 848313865, 3779631, 37234753, 69773345, 34, 0, 0, 0, 0, 8150637, 12554312, 10771),
    (147896334, 182205830, 147701158, 343020808, 173318316, 212870503, 45393028, 370315265, 137439488, 111185184, 2082, 0, 0, 0, 0, 0, 9238238, 1358197, 10800),
    (8010504, 108706600, 814750349, 40674304, 15827629, 548024367, 38798405, 102541868, 548407300, 649103460, 35907, 0, 0, 0, 0, 0, 14063592, 1754608, 15140),
    (276872207, 310779022, 345414830, 311629965, 174306561, 147096586, 302191872, 312644716, 11831362, 37792900, 3171, 0, 0, 0, 0, 0, 14253711, 10862614, 13490),
)


def split(x):
    high = x.astype(BF16)
    return high, (x - high.astype(F32)).astype(BF16)


def across_lanes(both, blocks):
    return [
        both[:, 2 * n * TOK : (2 * n + 1) * TOK] + both[:, (2 * n + 1) * TOK : 2 * (n + 1) * TOK]
        for n in range(blocks)
    ]


def attend(kv, slots, masks, first, q_ref, acc, top, total):
    keys, values = [], []
    for slot in slots:
        k_high, k_low = split(kv[slot, 0:TOK, :])
        keys += [jnp.concatenate([k_high, k_high], axis=1), jnp.concatenate([k_low, k_low], axis=1)]
        values.append(jnp.concatenate(split(kv[slot, KEY_ROWS:ROWS, :]), axis=1))
    keys, values = jnp.concatenate(keys, axis=0), jnp.concatenate(values, axis=0)
    both = lax.dot_general(
        q_ref[...], keys, (((1,), (1,)), ((), ())), preferred_element_type=F32
    )
    scores = [
        jnp.where(jnp.concatenate([mask] * HEADS, axis=0), score, MASKED)
        for mask, score in zip(masks, across_lanes(both, len(slots)))
    ]
    high = functools.reduce(jnp.maximum, scores)
    high = jnp.broadcast_to(jnp.max(high, axis=1, keepdims=True), high.shape)
    if not first:
        old = top[...]
        high = jnp.maximum(old, high)
        factor = jnp.exp2(old - high)
    top[...] = high
    weights = [jnp.exp2(score - high) for score in scores]
    added = functools.reduce(jnp.add, weights)
    w_high, w_low = zip(*[split(weight) for weight in weights])
    both = jnp.dot(jnp.concatenate(w_high, axis=1), values, preferred_element_type=F32)
    rest = jnp.dot(jnp.concatenate(w_low, axis=1), values[:, :TOK], preferred_element_type=F32)
    mixed = across_lanes(both, 1)[0] + rest
    total[...] = added if first else total[...] * factor + added
    acc[...] = mixed if first else acc[...] * factor + mixed


def kernel(
    planes, queries, keys, values, segment, out, kv, seg_raw, q_raw, q_ref, acc, top, total,
    load_sem, send_sem, recv_sem,
):
    inner, outer = lax.axis_index("inner"), lax.axis_index("outer")
    x, z = lax.div(inner, RING), lax.rem(inner, RING)
    plane, core = lax.div(outer, 2), lax.rem(outer, 2)
    up, down, across = lax.rem(z + 1, RING), lax.rem(z + RING - 1, RING), 1 - x
    ahead, behind = lax.rem(plane + 1, planes), lax.rem(plane + planes - 1, planes)
    far = planes // 2
    last = plane == planes - 1

    def at(to_plane, to_x, to_z, to_core):
        return {"inner": to_x * RING + to_z, "outer": to_plane * 2 + to_core}

    loads = [
        pltpu.make_async_copy(segment, seg_raw, load_sem.at[0]),
        pltpu.make_async_copy(keys, kv.at[OWN, pl.ds(0, TOK)], load_sem.at[1]),
        pltpu.make_async_copy(values, kv.at[OWN, pl.ds(KEY_ROWS, TOK)], load_sem.at[2]),
        pltpu.make_async_copy(queries, q_raw, load_sem.at[3]),
    ]
    for load in loads:
        load.start()

    barrier = pltpu.get_barrier_semaphore()

    def greet(device):
        pl.semaphore_signal(barrier, inc=1, device_id=device, device_id_type=MESH)

    for to_x, to_z in ((x, up), (x, down), (across, z)):
        for to_core in (0, 1):
            greet(at(plane, to_x, to_z, to_core))
    greet(at(plane, x, z, 1 - core))

    @pl.when(core == 0)
    def _():
        greet(at(behind, x, z, 0))
        greet(at(behind, x, z, 1))

    @pl.when((core == 0) & (x == 0))
    def _():
        greet(at(behind, 1, z, 1))

    def lookup(options, n, each, width):
        word, rest = lax.div(n, each), lax.rem(n, each)
        packed = options[0]
        for k in range(1, len(options)):
            packed = jnp.where(word == k, options[k], packed)
        field = lax.rem(packed, 1 << width)
        for k in range(1, each):
            field = jnp.where(
                rest == k, lax.rem(lax.div(packed, 1 << (width * k)), 1 << width), field
            )
        return field

    def event_of(n):
        return lookup(words[:16], n, 3, 10)

    def slot_of(n):
        return lookup(words[16:], n, 6, 4)

    def bit(event, place):
        return lax.rem(lax.div(event, 1 << place), 2) == 1

    def piece(held, slot, part, device, way):
        first, count = PARTS[part]
        return pltpu.make_async_remote_copy(
            src_ref=kv.at[held, pl.ds(first, count)],
            dst_ref=kv.at[slot, pl.ds(first, count)],
            send_sem=send_sem.at[way, held, part],
            recv_sem=recv_sem.at[slot, part],
            device_id=device,
            device_id_type=MESH,
        )


    def absent(slot):
        kept = (lax.div(slot, RING) == x) & (lax.rem(slot, RING) < z)
        same = lax.div(slot, RING) == x
        return (plane == 0) & (core == 0) & (slot < PASSING) & ~kept & (same | (x == 0))

    def direct(index):
        return ~last & ((plane != far - 1) | ((x == 1) & (lax.rem(index, 2) == 0)))

    def onward(event, part, act):
        held = lax.rem(event, 32)
        index, passing = lax.rem(held, RING), held >= PASSING
        crossed = (held < PASSING) & (lax.div(held, RING) != x)
        is_o = passing | (~crossed & (core == 1) & (index < z))
        here = x * RING + index
        there = ~absent(held)
        for way, to_z in ((0, up), (1, down)):
            below = index < to_z
            to_core = jnp.where(crossed, core, jnp.where(is_o == below, 1, 0))
            to_slot = jnp.where(is_o, jnp.where(below, here, PASSING + index), held)

            @pl.when(bit(event, 7 + way) & there)
            def _():
                act(piece(held, to_slot, part, at(plane, x, to_z, to_core), way))

        @pl.when(bit(event, 9) & ~(is_o & ~direct(index)))
        def _():
            aside = {
                "inner": jnp.where(is_o, inner, across * RING + z),
                "outer": jnp.where(is_o, ahead * 2, plane * 2 + x),
            }
            act(piece(held, here, part, aside, 2))

        from_near = (plane == far - 1) & (x == 1) & (core == 1)
        from_far = (plane == far) & (x == 0) & (core == 0) & (lax.rem(index, 2) == 1)

        @pl.when(crossed & (index >= z) & (from_near | from_far))
        def _():
            aside = {
                "inner": jnp.where(from_near, z, RING + z),
                "outer": far * 2,
            }
            act(piece(held, held, part, aside, 2))

    def own_onward(part, act):
        for way, to_z in ((0, up), (1, down)):
            hops = lax.rem(to_z - z + RING, RING)
            below = z < to_z
            to_core = jnp.where((core == 1) == below, 1, 0)
            to_slot = jnp.where((core == 1) & ~below, PASSING + z, inner)
            act(piece(OWN, to_slot, part, at(plane, x, to_z, to_core), way))

        @pl.when(core == 0)
        def _():
            act(piece(OWN, inner, part, at(plane, across, z, x), 2))
            act(piece(OWN, inner, part, at(plane, x, z, 1), 3))

        @pl.when((core == 1) & direct(z))
        def _():
            act(piece(OWN, inner, part, at(ahead, x, z, 0), 3))

        @pl.when((core == 1) & ((x == 0) | ~last))
        def _():
            crossing = {
                "inner": across * RING + z,
                "outer": jnp.where(x == 0, plane * 2 + 1, ahead * 2),
            }
            act(piece(OWN, inner, part, crossing, 2))

    def start(copy):
        copy.start()

    def finish(copy):
        copy.wait_send()

    loads[0].wait()
    own_seg = seg_raw[...].astype(F32)
    kv[OWN, TOK:KEY_ROWS, :] = jnp.broadcast_to(own_seg, (8, TOK))
    pl.semaphore_wait(barrier, 8 + core * x)
    for part in (0, 1):
        loads[1 + part].wait()
        own_onward(part, start)

    place = inner * 2 + core + jnp.where(plane == far, 2 * SLOTS, 0)
    words = [jnp.int32(0)] * 19
    for row, packed in enumerate(PLAN):
        words = [jnp.where(place == row, jnp.int32(p), w) for p, w in zip(packed, words)]

    loads[3].wait()
    scale = math.log2(math.e) / math.sqrt(TOK)
    for head in range(HEADS):
        rows = slice(head * TOK, (head + 1) * TOK)
        q_high, q_low = split(q_raw[:, rows] * scale)
        q_ref[rows, 0:TOK] = q_high
        q_ref[rows, TOK : 2 * TOK] = q_low

    row = lax.broadcasted_iota(jnp.int32, (TOK, TOK), 0)
    col = lax.broadcasted_iota(jnp.int32, (TOK, TOK), 1)
    seg_row = jnp.broadcast_to(own_seg, (TOK, TOK))
    seg_col = seg_row.T
    attend(kv, [OWN], [(seg_col == seg_row) & (col <= row)], True, q_ref, acc, top, total)

    lead = own_seg[:, 0:1]
    pieces = 2 * (SLOTS + (1 - core) * (RING - 1 - z))

    def pair(n):
        slots = [slot_of(2 * n), slot_of(2 * n + 1)]
        masks = []
        for slot in slots:
            seg = kv[slot, TOK : TOK + 1, :]
            shared = jnp.sum(jnp.where(seg == lead, 1.0, 0.0), axis=1, keepdims=True)
            masks.append((seg_col == lead) & (col.astype(F32) >= TOK - shared))
        attend(kv, slots, masks, False, q_ref, acc, top, total)

    def each_part(event, do):
        for part in (0, 1):

            @pl.when(bit(event, 5) == (part == 1))
            def _():
                do(part)

    def step(n, paired):
        event = event_of(n)

        def receive(part):
            slot = lax.rem(event, 32)
            first, count = PARTS[part]

            @pl.when(absent(slot))
            def _():
                kv[slot, first : first + count, :] = jnp.zeros((count, TOK), F32)
                if part == 0:
                    kv[slot, TOK:KEY_ROWS, :] = jnp.full((8, TOK), -1.0, F32)

            @pl.when(~absent(slot))
            def _():
                piece(slot, slot, part, at(plane, x, up, core), 0).wait_recv()
                onward(event, part, start)

        each_part(event, receive)
        now = bit(event, 6)

        @pl.when(now)
        def _():
            pair(paired)

        @pl.when(n >= LAG)
        def _():
            drain(n - LAG, 0)

        return paired + jnp.where(now, 1, 0)

    def drain(n, carry):
        event = event_of(n)

        crosses = (plane == far - 1) | (plane == far)

        @pl.when((event >= 1 << 7) | crosses)
        def _():
            each_part(event, lambda part: onward(event, part, finish))

        return carry

    paired = lax.fori_loop(0, pieces, step, jnp.int32(0))

    def rest(n, carry):
        pair(n)
        return carry

    lax.fori_loop(paired, SLOTS // 2, rest, 0)

    for head in range(HEADS):
        rows = slice(head * TOK, (head + 1) * TOK)
        out[:, rows] = acc[rows, :] / jnp.sum(total[rows, :], axis=1, keepdims=True)

    lax.fori_loop(pieces - LAG, pieces, drain, 0)
    for part in (0, 1):
        own_onward(part, finish)


def body(queries, keys, values, segment):
    planes = lax.axis_size("outer") // 2
    rows = HEADS * TOK
    return pl.pallas_call(
        functools.partial(kernel, planes),
        name="gather_and_attend",
        out_shape=pltpu.VMEM(queries.shape, F32),
        in_specs=[pl.BlockSpec(memory_space=pltpu.HBM)] * 4,
        out_specs=pl.BlockSpec(memory_space=pltpu.VMEM),
        scratch_shapes=[
            pltpu.VMEM((OWN + 1, ROWS, TOK), F32),
            pltpu.VMEM((1, TOK), jnp.int32),
            pltpu.VMEM((TOK, rows), F32),
            pltpu.VMEM((rows, 2 * TOK), BF16),
            pltpu.VMEM((rows, TOK), F32),
            pltpu.VMEM((rows, TOK), F32),
            pltpu.VMEM((rows, TOK), F32),
            pltpu.SemaphoreType.DMA((4,)),
            pltpu.SemaphoreType.DMA((4, OWN + 1, 2)),
            pltpu.SemaphoreType.DMA((OWN, 2)),
        ],
        compiler_params=pltpu.CompilerParams(
            collective_id=0, has_side_effects=True, vmem_limit_bytes=60 << 20
        ),
    )(queries, keys, values, segment.reshape(1, TOK))


def solution(mesh):
    return jax.shard_map(
        body,
        mesh=mesh,
        in_specs=(
            P(("outer", "inner"), None),
            P(("outer", "inner"), None),
            P(("outer", "inner"), None),
            P(("outer", "inner")),
        ),
        out_specs=P(("outer", "inner"), None),
        check_vma=False,
    )
```

```python
import functools
import math

import jax
import jax.numpy as jnp
from jax import lax
from jax.experimental import pallas as pl
from jax.experimental.pallas import tpu as pltpu
from jax.sharding import PartitionSpec as P

MESH = pl.DeviceIdType.MESH
F32, BF16 = jnp.float32, jnp.bfloat16

TOK = 128
HEADS = 8
RING = 8
SLOTS = 16
PASSING = SLOTS
OWN = SLOTS + RING
KEY_ROWS = TOK + 8
ROWS = KEY_ROWS + TOK
PARTS = ((0, KEY_ROWS), (KEY_ROWS, TOK))
UP_HOPS = (4, 3)
LAG = 12
MASKED = -1e30

PLAN = (
    (345014272, 311828481, 2596897, 217062666, 379624482, 39917743, 5388291, 249572387, 214996267, 4305956, 45068, 0, 0, 0, 0, 0, 7504272, 12465914, 50389),
    (840779521, 100664113, 695869186, 711992082, 42764983, 10099506, 43519638, 727722662, 49826831, 111971973, 693123891, 48796683, 45617781, 591476260, 46249556, 12, 9971457, 15049718, 52555),
    (412189697, 2818473, 346065568, 3285290, 280005864, 71609351, 12729383, 183507044, 148937068, 38844421, 13421, 0, 0, 0, 0, 0, 9052305, 13584307, 54758),
    (807502849, 43796489, 11389730, 44829824, 9194720, 678470435, 695217971, 779637316, 45801252, 745328655, 49960972, 15260262, 558936613, 609270325, 13357, 0, 3187345, 7320696, 54764),
    (705694401, 144058466, 3319210, 280006336, 313529056, 281223204, 176166188, 38870029, 41106733, 6405158, 14382, 0, 0, 0, 0, 0, 236065, 13995083, 59127),
    (135366658, 11275489, 842050323, 43001715, 826289924, 843251755, 12813108, 558899717, 46961704, 861560519, 661665319, 543725583, 594040941, 14727215, 0, 0, 12139026, 8148996, 61398),
    (3836610, 414909475, 4632225, 178398410, 671191308, 244323628, 282170912, 142612781, 316774414, 7380072, 48143, 0, 0, 0, 0, 0, 4895026, 7164060, 63374),
    (203459587, 827068578, 45220875, 236770084, 827337477, 844116010, 928034825, 543175721, 114841728, 8422182, 544291638, 48798824, 83418711, 47, 0, 0, 10570531, 448965, 65144),
    (37753475, 740700899, 73042348, 282105473, 6849675, 144944493, 283255846, 7864554, 570533166, 8469543, 41263, 0, 0, 0, 0, 0, 1387572, 10397373, 36720),
    (137465860, 171726597, 861705228, 811796524, 828540939, 845196365, 862061613, 544225354, 628130858, 116169737, 43073335, 116424704, 40968, 0, 0, 0, 11715892, 15145686, 36617),
    (38803076, 741750500, 774904237, 283154572, 537047682, 384337927, 906495015, 317926671, 571649162, 75540553, 303145, 0, 0, 0, 0, 0, 12991813, 12519394, 35233),
    (138515461, 14441222, 48011428, 812781430, 171727884, 46963726, 12442670, 81026, 116426795, 77595936, 8487978, 43032649, 0, 0, 0, 0, 7591493, 994284, 38938),
    (39852677, 742800101, 7781120, 148669156, 351931431, 317896193, 539788899, 277032969, 312051884, 77897867, 43051, 0, 0, 0, 0, 0, 7360086, 2888701, 43913),
    (139565062, 173825799, 862993191, 268636206, 171981837, 116438304, 1182732, 36745288, 78749985, 35660802, 10595433, 42, 0, 0, 0, 0, 321366, 8469757, 43922),
    (8002304, 778862631, 874124687, 907711919, 675494153, 182723074, 148219428, 540903720, 312718346, 46281315, 11307, 0, 0, 0, 0, 0, 1439239, 13797710, 48186),
    (268540935, 302005382, 269597862, 14753925, 109348005, 138425454, 43000834, 104903970, 3158090, 44150819, 44043, 0, 0, 0, 0, 0, 1439239, 5057000, 47811),
    (837457, 695238664, 729630760, 1886217, 694191145, 10487823, 727759879, 556836903, 6371362, 3823411, 78682158, 36744757, 557847565, 37852788, 113315885, 12, 8329600, 3894826, 50389),
    (9217865, 816120872, 303709568, 917159328, 141888142, 786729483, 918172839, 584060038, 583178595, 38934092, 4132, 0, 0, 0, 0, 0, 11469193, 4044770, 17862),
    (34677761, 858540137, 11149314, 44075688, 696011840, 71093280, 557878283, 16505899, 5033991, 116432534, 593530892, 46143502, 107501109, 47298597, 13317, 0, 665745, 12908467, 54758),
    (403809289, 849839882, 304226562, 918367400, 687082624, 720536076, 753709411, 585243652, 584228196, 38935117, 5158, 0, 0, 0, 0, 0, 12069401, 5161968, 22231),
    (10488521, 111184553, 102517761, 11538227, 826314376, 4956203, 12583732, 46235684, 5987861, 7921461, 15766541, 40941078, 107599919, 14727174, 0, 0, 11737641, 14008392, 59127),
    (143763466, 438543746, 168953611, 818155371, 851807368, 550768872, 687116416, 586384173, 307771461, 41033326, 6182, 0, 0, 0, 0, 0, 3871386, 15783052, 26597),
    (715132618, 37364747, 2207508, 781224756, 1052684, 35410988, 861544548, 38810629, 67656296, 861935661, 39860320, 594655767, 49323023, 7, 0, 0, 13183802, 886081, 32742),
    (211856395, 885394602, 851584419, 177475778, 135498509, 919766308, 274217096, 853841000, 6831296, 653295910, 39943, 0, 0, 0, 0, 0, 2737067, 15043860, 32518),
    (79696523, 827364011, 3811436, 715134773, 2176035, 47224598, 6326985, 1063734, 34708009, 7453207, 41427831, 578813967, 32879, 0, 0, 0, 5483595, 14772525, 3975),
    (145862668, 180106628, 212710820, 820160773, 853906563, 552740067, 43260034, 854721894, 7374050, 309436424, 32768, 0, 0, 0, 0, 0, 5952700, 3107134, 1921),
    (80746124, 828413612, 4861037, 14687030, 830123108, 115382275, 8005667, 16262007, 69246506, 546356224, 579963688, 34604128, 0, 0, 0, 0, 7032156, 9402942, 4242),
    (146912269, 181156229, 146651557, 341971727, 239376555, 8530799, 44309635, 309497192, 43124809, 67143681, 294945, 0, 0, 0, 0, 0, 7071181, 7572212, 297),
    (81795725, 40656557, 684514414, 8134661, 717329423, 847297575, 682623044, 613449828, 649070377, 547392515, 580913249, 34, 0, 0, 0, 0, 8150637, 12125327, 10771),
    (147961870, 181803791, 214810022, 275911944, 240427180, 212870439, 112501892, 268436644, 302351370, 111185027, 2082, 0, 0, 0, 0, 0, 9238238, 1358197, 10800),
    (8010504, 720150607, 684833831, 7087168, 40674336, 1054445, 750818826, 583012449, 38643714, 649103883, 35843, 0, 0, 0, 0, 0, 9500648, 11277782, 15140),
    (276937743, 310779022, 278371502, 311564493, 174392493, 10629376, 302126369, 312644716, 78940226, 37792900, 3171, 0, 0, 0, 0, 0, 14253711, 10862614, 13490),
    (311828809, 1321448, 305295, 100697327, 2108558, 7646382, 147949574, 46248998, 72364071, 105942019, 4132, 0, 0, 0, 0, 0, 129673, 8217278, 17724),
    (840779521, 100664113, 824189698, 695247495, 712804361, 857843383, 78273158, 540032678, 556842678, 676345962, 842683403, 859346030, 541175349, 558469133, 47763500, 12, 9906177, 6175478, 52555),
    (671589769, 278922912, 2467937, 176195720, 150252875, 36707331, 381860876, 48380007, 4240390, 107057165, 37893, 0, 0, 0, 0, 0, 8560905, 15191867, 22093),
    (9536513, 892078121, 11324194, 167880832, 825238275, 12356712, 541728563, 16274071, 843099815, 859845303, 694206086, 82352172, 48880165, 626578949, 13421, 0, 8430225, 13585267, 54758),
    (413828801, 177350122, 36306946, 381387019, 281157635, 381853731, 315634692, 116429007, 48241669, 40974373, 6182, 0, 0, 0, 0, 0, 11544993, 16047235, 26597),
    (135366658, 111313930, 826018825, 926714921, 827068427, 843251755, 859996172, 542154824, 844715052, 861560455, 14261263, 543743526, 47765551, 48249430, 0, 0, 11770386, 7718916, 60918),
    (672828098, 448147169, 143894666, 177483779, 381718144, 282071648, 15053860, 5283976, 49657893, 39917583, 7207, 0, 0, 0, 0, 0, 3779346, 5821452, 30462),
    (203459587, 809512098, 11358251, 859965220, 12747818, 10245957, 43881516, 201340725, 47733254, 9279520, 544291638, 628144168, 595106831, 47, 0, 0, 1723171, 6347100, 63464),
    (415928003, 707244674, 282071681, 315723915, 144879201, 178263310, 316810277, 638058601, 317724687, 42016806, 40007, 0, 0, 0, 0, 0, 1917635, 648619, 30831),
    (137465860, 46928908, 844271381, 137221131, 829167629, 47351851, 14691174, 44173110, 561035847, 101721895, 110182199, 100663343, 40968, 0, 0, 0, 2839492, 1567341, 33017),
    (416977604, 708294275, 283120780, 247502466, 640155950, 605847558, 146029606, 571649327, 9480394, 108076040, 303145, 0, 0, 0, 0, 0, 15487956, 1832450, 35194),
    (138515461, 828389126, 845320237, 137376566, 830282766, 48401452, 15740775, 112331639, 67143727, 1343498, 34646088, 43000936, 0, 0, 0, 0, 3957973, 195454, 38938),
    (418027205, 872856196, 148734628, 674511878, 181928998, 907578735, 9580551, 276864514, 312051948, 377531531, 43018, 0, 0, 0, 0, 0, 14025957, 2912575, 43193),
    (14784518, 830217349, 846369902, 15742775, 47448196, 369147044, 137437196, 109052972, 78939171, 2139209, 10520683, 42, 0, 0, 0, 0, 5076454, 1281039, 41657),
    (711787142, 676740960, 710328065, 278018913, 539627527, 277067815, 310748708, 540838029, 379827210, 46763148, 11307, 0, 0, 0, 0, 0, 7429894, 13797710, 48186),
    (140614663, 116654095, 75792550, 269620238, 173062184, 9516321, 138454018, 77631597, 3508236, 36808748, 44043, 0, 0, 0, 0, 0, 15206135, 2414869, 45996),
    (837457, 824214167, 1886903, 77223969, 556802050, 858791606, 693215273, 108038154, 44618758, 591477798, 49827843, 36711429, 4232270, 112244772, 46248973, 12, 7506192, 4538218, 52670),
    (9217865, 816055400, 303432335, 916882095, 304417422, 786967687, 752659623, 584060038, 241471020, 38934092, 4132, 0, 0, 0, 0, 0, 10547593, 4044770, 17862),
    (824214593, 2761522, 36347913, 892338281, 859462688, 44043274, 8052308, 37378868, 40898571, 104902198, 40391750, 38813237, 46251020, 48314373, 13357, 0, 10523265, 16141171, 56924),
    (403809289, 849839882, 304226562, 918367400, 134754959, 235584771, 753176364, 585109639, 550801639, 39983725, 5157, 0, 0, 0, 0, 0, 12069401, 8272911, 22228),
    (714083017, 825230434, 11324449, 44043912, 104506132, 926941188, 695217184, 112235029, 860886028, 46145079, 594106405, 39859303, 15840262, 14727215, 0, 0, 3711273, 7719744, 61398),
    (210806794, 438543746, 168953611, 272380779, 176992392, 687149411, 134517261, 168410925, 552122437, 41098533, 6182, 0, 0, 0, 0, 0, 13308570, 1037368, 26462),
    (3844810, 104616585, 2937513, 827327586, 34614276, 38590088, 5873707, 79730198, 114087936, 561001504, 114333702, 40909367, 15775815, 47, 0, 0, 4270394, 6342027, 65149),
    (211856395, 473706666, 507293833, 177475714, 135498509, 919766308, 274217096, 308066408, 134224463, 375423535, 39943, 0, 0, 0, 0, 0, 2702507, 6196500, 30223),
    (716247691, 682447908, 6083587, 38899370, 680538902, 929083394, 103326726, 1596454, 863024141, 7354401, 108569096, 100728878, 48143, 0, 0, 0, 12925515, 8508969, 61671),
    (145862668, 180106628, 145601956, 178526030, 308131971, 552832137, 43124998, 308448047, 7374017, 106568, 33063, 0, 0, 0, 0, 0, 15389884, 6486325, 1921),
    (717297292, 682727190, 6296374, 830123044, 3224614, 48029322, 7907848, 847289443, 69739534, 566318, 1148943, 34651168, 0, 0, 0, 0, 14070876, 10389306, 7938),
    (146912269, 180754190, 146249518, 341971727, 172801195, 8595814, 137632810, 309339432, 43124963, 1048674, 295009, 0, 0, 0, 0, 0, 16473805, 3639908, 297),
    (829495949, 863083181, 813700748, 717263879, 82616359, 116009988, 38282240, 649102121, 547425295, 36813825, 2197034, 34, 0, 0, 0, 0, 8897901, 16451918, 8611),
    (821147662, 854988941, 147298477, 343020808, 173318316, 212870503, 45393028, 335712257, 302000417, 103852227, 2082, 0, 0, 0, 0, 0, 9203198, 1358197, 9120),
    (75119368, 108706600, 814750349, 40674304, 15827629, 683677194, 38845505, 849380908, 548409410, 649168996, 35843, 0, 0, 0, 0, 0, 14063592, 10601968, 15140),
    (276937743, 310779022, 345414830, 311629965, 174306561, 147062794, 369235233, 312644716, 11831362, 37949483, 3107, 0, 0, 0, 0, 0, 14253711, 10862614, 13490),
)


def split(x):
    high = x.astype(BF16)
    return high, (x - high.astype(F32)).astype(BF16)


def across_lanes(both, blocks):
    return [
        both[:, 2 * n * TOK : (2 * n + 1) * TOK] + both[:, (2 * n + 1) * TOK : 2 * (n + 1) * TOK]
        for n in range(blocks)
    ]


def attend(kv, slots, masks, first, q_ref, acc, top, total):
    keys, values = [], []
    for slot in slots:
        k_high, k_low = split(kv[slot, 0:TOK, :])
        keys += [jnp.concatenate([k_high, k_high], axis=1), jnp.concatenate([k_low, k_low], axis=1)]
        values.append(jnp.concatenate(split(kv[slot, KEY_ROWS:ROWS, :]), axis=1))
    keys, values = jnp.concatenate(keys, axis=0), jnp.concatenate(values, axis=0)
    both = lax.dot_general(
        q_ref[...], keys, (((1,), (1,)), ((), ())), preferred_element_type=F32
    )
    scores = [
        jnp.where(jnp.concatenate([mask] * HEADS, axis=0), score, MASKED)
        for mask, score in zip(masks, across_lanes(both, len(slots)))
    ]
    high = functools.reduce(jnp.maximum, scores)
    high = jnp.broadcast_to(jnp.max(high, axis=1, keepdims=True), high.shape)
    if not first:
        old = top[...]
        high = jnp.maximum(old, high)
        factor = jnp.exp2(old - high)
    top[...] = high
    weights = [jnp.exp2(score - high) for score in scores]
    added = functools.reduce(jnp.add, weights)
    w_high, w_low = zip(*[split(weight) for weight in weights])
    both = jnp.dot(jnp.concatenate(w_high, axis=1), values, preferred_element_type=F32)
    rest = jnp.dot(jnp.concatenate(w_low, axis=1), values[:, :TOK], preferred_element_type=F32)
    mixed = across_lanes(both, 1)[0] + rest
    total[...] = added if first else total[...] * factor + added
    acc[...] = mixed if first else acc[...] * factor + mixed


def kernel(
    planes, queries, keys, values, segment, out, kv, seg_raw, q_raw, q_ref, acc, top, total,
    load_sem, send_sem, recv_sem,
):
    inner, outer = lax.axis_index("inner"), lax.axis_index("outer")
    x, z = lax.div(inner, RING), lax.rem(inner, RING)
    plane, core = lax.div(outer, 2), lax.rem(outer, 2)
    up, down, across = lax.rem(z + 1, RING), lax.rem(z + RING - 1, RING), 1 - x
    ahead, behind = lax.rem(plane + 1, planes), lax.rem(plane + planes - 1, planes)
    far = planes // 2

    def at(to_plane, to_x, to_z, to_core):
        return {"inner": to_x * RING + to_z, "outer": to_plane * 2 + to_core}

    loads = [
        pltpu.make_async_copy(segment, seg_raw, load_sem.at[0]),
        pltpu.make_async_copy(keys, kv.at[OWN, pl.ds(0, TOK)], load_sem.at[1]),
        pltpu.make_async_copy(values, kv.at[OWN, pl.ds(KEY_ROWS, TOK)], load_sem.at[2]),
        pltpu.make_async_copy(queries, q_raw, load_sem.at[3]),
    ]
    for load in loads:
        load.start()

    barrier = pltpu.get_barrier_semaphore()

    def greet(device):
        pl.semaphore_signal(barrier, inc=1, device_id=device, device_id_type=MESH)

    for to_x, to_z in ((x, up), (x, down), (across, z)):
        for to_core in (0, 1):
            greet(at(plane, to_x, to_z, to_core))
    greet(at(plane, x, z, 1 - core))

    @pl.when(core == 0)
    def _():
        greet(at(behind, x, z, 0))
        greet(at(behind, x, z, 1))

    @pl.when((core == 0) & (x == 0))
    def _():
        greet(at(behind, 1, z, 1))

    def lookup(options, n, each, width):
        word, rest = lax.div(n, each), lax.rem(n, each)
        packed = options[0]
        for k in range(1, len(options)):
            packed = jnp.where(word == k, options[k], packed)
        field = lax.rem(packed, 1 << width)
        for k in range(1, each):
            field = jnp.where(
                rest == k, lax.rem(lax.div(packed, 1 << (width * k)), 1 << width), field
            )
        return field

    def event_of(n):
        return lookup(words[:16], n, 3, 10)

    def slot_of(n):
        return lookup(words[16:], n, 6, 4)

    def bit(event, place):
        return lax.rem(lax.div(event, 1 << place), 2) == 1

    def piece(held, slot, part, device, way):
        first, count = PARTS[part]
        return pltpu.make_async_remote_copy(
            src_ref=kv.at[held, pl.ds(first, count)],
            dst_ref=kv.at[slot, pl.ds(first, count)],
            send_sem=send_sem.at[way, held, part],
            recv_sem=recv_sem.at[slot, part],
            device_id=device,
            device_id_type=MESH,
        )


    def absent(slot):
        kept = (lax.div(slot, RING) == x) & (lax.rem(slot, RING) < z)
        same = lax.div(slot, RING) == x
        return (plane == 0) & (core == 0) & (slot < PASSING) & ~kept & (same | (x == 0))

    def straight(to_x, hops):
        low = jnp.where(to_x == 0, 4, 2)
        return (hops >= low) & (hops <= low + 2)

    def direct(index):
        return (plane != planes - 1) & ((plane != far - 1) | straight(x, index - z))

    def onward(event, part, act):
        held = lax.rem(event, 32)
        index, passing = lax.rem(held, RING), held >= PASSING
        crossed = (held < PASSING) & (lax.div(held, RING) != x)
        is_o = passing | (~crossed & (core == 1) & (index < z))
        here = x * RING + index
        there = ~absent(held)
        for way, to_z in ((0, up), (1, down)):
            below = index < to_z
            to_core = jnp.where(below, jnp.where(is_o, 1, 0), jnp.where(is_o, across, 1))
            to_core = jnp.where(crossed, core, to_core)
            to_slot = jnp.where(is_o, jnp.where(below, here, PASSING + index), held)

            @pl.when(bit(event, 7 + way) & there)
            def _():
                act(piece(held, to_slot, part, at(plane, x, to_z, to_core), way))

        @pl.when(bit(event, 9) & ~(is_o & ~direct(index)))
        def _():
            aside = {
                "inner": jnp.where(is_o, inner, across * RING + z),
                "outer": jnp.where(is_o, ahead * 2, plane * 2 + x),
            }
            act(piece(held, here, part, aside, 2))

        from_near = (plane == far - 1) & (x == 1) & (core == 1)
        from_far = (plane == far) & (x == 0) & (core == 0)
        to_x = jnp.where(from_near, 0, 1)

        @pl.when(crossed & (index >= z) & (from_near | from_far) & ~straight(to_x, index - z))
        def _():
            act(piece(held, held, part, at(far, to_x, z, 0), 2))

    def own_onward(part, act):
        for way, to_z in ((0, up), (1, down)):
            hops = lax.rem(to_z - z + RING, RING)
            below = z < to_z
            to_core = jnp.where(below, core, jnp.where(core == 1, across, 1))
            to_slot = jnp.where((core == 1) & ~below, PASSING + z, inner)
            act(piece(OWN, to_slot, part, at(plane, x, to_z, to_core), way))

        @pl.when(core == 0)
        def _():
            act(piece(OWN, inner, part, at(plane, across, z, x), 2))
            act(piece(OWN, inner, part, at(plane, x, z, 1), 3))

        @pl.when((core == 1) & direct(z))
        def _():
            act(piece(OWN, inner, part, at(ahead, x, z, 0), 3))

        @pl.when((core == 1) & ((x == 0) | (plane != planes - 1)))
        def _():
            crossing = {
                "inner": across * RING + z,
                "outer": jnp.where(x == 0, plane * 2 + 1, ahead * 2),
            }
            act(piece(OWN, inner, part, crossing, 2))

    def start(copy):
        copy.start()

    def finish(copy):
        copy.wait_send()

    loads[0].wait()
    own_seg = seg_raw[...].astype(F32)
    kv[OWN, TOK:KEY_ROWS, :] = jnp.broadcast_to(own_seg, (8, TOK))
    pl.semaphore_wait(barrier, 8 + core * x)
    for part in (0, 1):
        loads[1 + part].wait()
        own_onward(part, start)

    place = inner * 2 + core + jnp.where(plane == far, 2 * SLOTS, 0)
    words = [jnp.int32(0)] * 19
    for row, packed in enumerate(PLAN):
        words = [jnp.where(place == row, jnp.int32(p), w) for p, w in zip(packed, words)]

    lead = own_seg[:, 0:1]
    pieces = 2 * (SLOTS + jnp.where(core == across, RING - 1 - z, 0))

    row = lax.broadcasted_iota(jnp.int32, (TOK, TOK), 0)
    col = lax.broadcasted_iota(jnp.int32, (TOK, TOK), 1)
    seg_row = jnp.broadcast_to(own_seg, (TOK, TOK))
    seg_col = seg_row.T

    def alone():
        scale = math.log2(math.e) / math.sqrt(TOK)
        for head in range(HEADS):
            rows = slice(head * TOK, (head + 1) * TOK)
            q_high, q_low = split(q_raw[:, rows] * scale)
            q_ref[rows, 0:TOK] = q_high
            q_ref[rows, TOK : 2 * TOK] = q_low

        attend(kv, [OWN], [(seg_col == seg_row) & (col <= row)], True, q_ref, acc, top, total)

    def pair(n):
        slots = [slot_of(2 * n), slot_of(2 * n + 1)]
        masks = []
        for slot in slots:
            seg = kv[slot, TOK : TOK + 1, :]
            shared = jnp.sum(jnp.where(seg == lead, 1.0, 0.0), axis=1, keepdims=True)
            masks.append((seg_col == lead) & (col.astype(F32) >= TOK - shared))
        attend(kv, slots, masks, False, q_ref, acc, top, total)

    def each_part(event, do):
        for part in (0, 1):

            @pl.when(bit(event, 5) == (part == 1))
            def _():
                do(part)

    def turn(done):
        @pl.when(done == 0)
        def _():
            alone()

        @pl.when(done > 0)
        def _():
            pair(done - 1)

    def step(n, done):
        event = event_of(n)

        def receive(part):
            slot = lax.rem(event, 32)
            first, count = PARTS[part]

            @pl.when(absent(slot))
            def _():
                kv[slot, first : first + count, :] = jnp.zeros((count, TOK), F32)
                if part == 0:
                    kv[slot, TOK:KEY_ROWS, :] = jnp.full((8, TOK), -1.0, F32)

            @pl.when(~absent(slot))
            def _():
                piece(slot, slot, part, at(plane, x, up, core), 0).wait_recv()
                onward(event, part, start)

        each_part(event, receive)
        now = bit(event, 6)

        @pl.when(now)
        def _():
            turn(done)

        @pl.when(n >= LAG)
        def _():
            drain(n - LAG, 0)

        return done + jnp.where(now, 1, 0)

    def drain(n, carry):
        event = event_of(n)

        crosses = (plane == far - 1) | (plane == far)

        @pl.when((event >= 1 << 7) | crosses)
        def _():
            each_part(event, lambda part: onward(event, part, finish))

        return carry

    loads[3].wait()
    done = lax.fori_loop(0, pieces, step, jnp.int32(0))

    def rest(n, carry):
        turn(n)
        return carry

    lax.fori_loop(done, SLOTS // 2 + 1, rest, 0)

    for head in range(HEADS):
        rows = slice(head * TOK, (head + 1) * TOK)
        out[:, rows] = acc[rows, :] / jnp.sum(total[rows, :], axis=1, keepdims=True)

    lax.fori_loop(pieces - LAG, pieces, drain, 0)
    for part in (0, 1):
        own_onward(part, finish)


def body(queries, keys, values, segment):
    planes = lax.axis_size("outer") // 2
    rows = HEADS * TOK
    return pl.pallas_call(
        functools.partial(kernel, planes),
        name="gather_and_attend",
        out_shape=pltpu.VMEM(queries.shape, F32),
        in_specs=[pl.BlockSpec(memory_space=pltpu.HBM)] * 4,
        out_specs=pl.BlockSpec(memory_space=pltpu.VMEM),
        scratch_shapes=[
            pltpu.VMEM((OWN + 1, ROWS, TOK), F32),
            pltpu.VMEM((1, TOK), jnp.int32),
            pltpu.VMEM((TOK, rows), F32),
            pltpu.VMEM((rows, 2 * TOK), BF16),
            pltpu.VMEM((rows, TOK), F32),
            pltpu.VMEM((rows, TOK), F32),
            pltpu.VMEM((rows, TOK), F32),
            pltpu.SemaphoreType.DMA((4,)),
            pltpu.SemaphoreType.DMA((4, OWN + 1, 2)),
            pltpu.SemaphoreType.DMA((OWN, 2)),
        ],
        compiler_params=pltpu.CompilerParams(
            collective_id=0, has_side_effects=True, vmem_limit_bytes=60 << 20
        ),
    )(queries, keys, values, segment.reshape(1, TOK))


def solution(mesh):
    return jax.shard_map(
        body,
        mesh=mesh,
        in_specs=(
            P(("outer", "inner"), None),
            P(("outer", "inner"), None),
            P(("outer", "inner"), None),
            P(("outer", "inner")),
        ),
        out_specs=P(("outer", "inner"), None),
        check_vma=False,
    )
```

```python
import functools
import math

import jax
import jax.numpy as jnp
from jax import lax
from jax.experimental import pallas as pl
from jax.experimental.pallas import tpu as pltpu
from jax.sharding import PartitionSpec as P

MESH = pl.DeviceIdType.MESH
F32, BF16 = jnp.float32, jnp.bfloat16

TOK = 128
HEADS = 8
RING = 8
SLOTS = 16
PASSING = SLOTS
OWN = SLOTS + RING
KEY_ROWS = TOK + 8
ROWS = KEY_ROWS + TOK
PARTS = ((0, TOK), (TOK, ROWS - TOK))
UP_HOPS = (4, 3)
LAG = 12
MASKED = -1e30

PLAN = (
    (345014272, 311828481, 2596897, 217062666, 379624482, 39917743, 5388291, 249572387, 214996267, 4305956, 45068, 0, 0, 0, 0, 0, 7504272, 12465914, 50389),
    (840779521, 100664113, 695869186, 711992082, 42764983, 10099506, 43519638, 727722662, 49826831, 111971973, 693123891, 48796683, 45617781, 591476260, 46249556, 12, 9971457, 15049718, 52555),
    (412189697, 2818473, 346065568, 3285290, 280005864, 71609351, 12729383, 183507044, 148937068, 38844421, 13421, 0, 0, 0, 0, 0, 9052305, 13584307, 54758),
    (807502849, 43796489, 11389730, 44829824, 9194720, 678470435, 695217971, 779637316, 45801252, 745328655, 49960972, 15260262, 558936613, 609270325, 13357, 0, 3187345, 7320696, 54764),
    (705694401, 144058466, 3319210, 280006336, 313529056, 281223204, 176166188, 38870029, 41106733, 6405158, 14382, 0, 0, 0, 0, 0, 236065, 13995083, 59127),
    (135366658, 11275489, 842050323, 43001715, 826289924, 843251755, 12813108, 558899717, 46961704, 861560519, 661665319, 543725583, 594040941, 14727215, 0, 0, 12139026, 8148996, 61398),
    (3836610, 414909475, 4632225, 178398410, 671191308, 244323628, 282170912, 142612781, 316774414, 7380072, 48143, 0, 0, 0, 0, 0, 4895026, 7164060, 63374),
    (203459587, 827068578, 45220875, 236770084, 827337477, 844116010, 928034825, 543175721, 114841728, 8422182, 544291638, 48798824, 83418711, 47, 0, 0, 10570531, 448965, 65144),
    (37753475, 740700899, 73042348, 282105473, 6849675, 144944493, 283255846, 7864554, 570533166, 8469543, 41263, 0, 0, 0, 0, 0, 1387572, 10397373, 36720),
    (137465860, 171726597, 861705228, 811796524, 828540939, 845196365, 862061613, 544225354, 628130858, 116169737, 43073335, 116424704, 40968, 0, 0, 0, 11715892, 15145686, 36617),
    (38803076, 741750500, 774904237, 283154572, 537047682, 384337927, 906495015, 317926671, 571649162, 75540553, 303145, 0, 0, 0, 0, 0, 12991813, 12519394, 35233),
    (138515461, 14441222, 48011428, 812781430, 171727884, 46963726, 12442670, 81026, 116426795, 77595936, 8487978, 43032649, 0, 0, 0, 0, 7591493, 994284, 38938),
    (39852677, 742800101, 7781120, 148669156, 351931431, 317896193, 539788899, 277032969, 312051884, 77897867, 43051, 0, 0, 0, 0, 0, 7360086, 2888701, 43913),
    (139565062, 173825799, 862993191, 268636206, 171981837, 116438304, 1182732, 36745288, 78749985, 35660802, 10595433, 42, 0, 0, 0, 0, 321366, 8469757, 43922),
    (8002304, 778862631, 874124687, 907711919, 675494153, 182723074, 148219428, 540903720, 312718346, 46281315, 11307, 0, 0, 0, 0, 0, 1439239, 13797710, 48186),
    (268540935, 302005382, 269597862, 14753925, 109348005, 138425454, 43000834, 104903970, 3158090, 44150819, 44043, 0, 0, 0, 0, 0, 1439239, 5057000, 47811),
    (837457, 695238664, 729630760, 1886217, 694191145, 10487823, 727759879, 556836903, 6371362, 3823411, 78682158, 36744757, 557847565, 37852788, 113315885, 12, 8329600, 3894826, 50389),
    (9217865, 816120872, 303709568, 917159328, 141888142, 786729483, 918172839, 584060038, 583178595, 38934092, 4132, 0, 0, 0, 0, 0, 11469193, 4044770, 17862),
    (34677761, 858540137, 11149314, 44075688, 696011840, 71093280, 557878283, 16505899, 5033991, 116432534, 593530892, 46143502, 107501109, 47298597, 13317, 0, 665745, 12908467, 54758),
    (403809289, 849839882, 304226562, 918367400, 687082624, 720536076, 753709411, 585243652, 584228196, 38935117, 5158, 0, 0, 0, 0, 0, 12069401, 5161968, 22231),
    (10488521, 111184553, 102517761, 11538227, 826314376, 4956203, 12583732, 46235684, 5987861, 7921461, 15766541, 40941078, 107599919, 14727174, 0, 0, 11737641, 14008392, 59127),
    (143763466, 438543746, 168953611, 818155371, 851807368, 550768872, 687116416, 586384173, 307771461, 41033326, 6182, 0, 0, 0, 0, 0, 3871386, 15783052, 26597),
    (715132618, 37364747, 2207508, 781224756, 1052684, 35410988, 861544548, 38810629, 67656296, 861935661, 39860320, 594655767, 49323023, 7, 0, 0, 13183802, 886081, 32742),
    (211856395, 885394602, 851584419, 177475778, 135498509, 919766308, 274217096, 853841000, 6831296, 653295910, 39943, 0, 0, 0, 0, 0, 2737067, 15043860, 32518),
    (79696523, 827364011, 3811436, 715134773, 2176035, 47224598, 6326985, 1063734, 34708009, 7453207, 41427831, 578813967, 32879, 0, 0, 0, 5483595, 14772525, 3975),
    (145862668, 180106628, 212710820, 820160773, 853906563, 552740067, 43260034, 854721894, 7374050, 309436424, 32768, 0, 0, 0, 0, 0, 5952700, 3107134, 1921),
    (80746124, 828413612, 4861037, 14687030, 830123108, 115382275, 8005667, 16262007, 69246506, 546356224, 579963688, 34604128, 0, 0, 0, 0, 7032156, 9402942, 4242),
    (146912269, 181156229, 146651557, 341971727, 239376555, 8530799, 44309635, 309497192, 43124809, 67143681, 294945, 0, 0, 0, 0, 0, 7071181, 7572212, 297),
    (81795725, 40656557, 684514414, 8134661, 717329423, 847297575, 682623044, 613449828, 649070377, 547392515, 580913249, 34, 0, 0, 0, 0, 8150637, 12125327, 10771),
    (147961870, 181803791, 214810022, 275911944, 240427180, 212870439, 112501892, 268436644, 302351370, 111185027, 2082, 0, 0, 0, 0, 0, 9238238, 1358197, 10800),
    (8010504, 720150607, 684833831, 7087168, 40674336, 1054445, 750818826, 583012449, 38643714, 649103883, 35843, 0, 0, 0, 0, 0, 9500648, 11277782, 15140),
    (276937743, 310779022, 278371502, 311564493, 174392493, 10629376, 302126369, 312644716, 78940226, 37792900, 3171, 0, 0, 0, 0, 0, 14253711, 10862614, 13490),
    (311828809, 1321448, 305295, 100697327, 2108558, 7646382, 147949574, 46248998, 72364071, 105942019, 4132, 0, 0, 0, 0, 0, 129673, 8217278, 17724),
    (840779521, 100664113, 824189698, 695247495, 712804361, 857843383, 78273158, 540032678, 556842678, 676345962, 842683403, 859346030, 541175349, 558469133, 47763500, 12, 9906177, 6175478, 52555),
    (671589769, 278922912, 2467937, 176195720, 150252875, 36707331, 381860876, 48380007, 4240390, 107057165, 37893, 0, 0, 0, 0, 0, 8560905, 15191867, 22093),
    (9536513, 892078121, 11324194, 167880832, 825238275, 12356712, 541728563, 16274071, 843099815, 859845303, 694206086, 82352172, 48880165, 626578949, 13421, 0, 8430225, 13585267, 54758),
    (413828801, 177350122, 36306946, 381387019, 281157635, 381853731, 315634692, 116429007, 48241669, 40974373, 6182, 0, 0, 0, 0, 0, 11544993, 16047235, 26597),
    (135366658, 111313930, 826018825, 926714921, 827068427, 843251755, 859996172, 542154824, 844715052, 861560455, 14261263, 543743526, 47765551, 48249430, 0, 0, 11770386, 7718916, 60918),
    (672828098, 448147169, 143894666, 177483779, 381718144, 282071648, 15053860, 5283976, 49657893, 39917583, 7207, 0, 0, 0, 0, 0, 3779346, 5821452, 30462),
    (203459587, 809512098, 11358251, 859965220, 12747818, 10245957, 43881516, 201340725, 47733254, 9279520, 544291638, 628144168, 595106831, 47, 0, 0, 1723171, 6347100, 63464),
    (415928003, 707244674, 282071681, 315723915, 144879201, 178263310, 316810277, 638058601, 317724687, 42016806, 40007, 0, 0, 0, 0, 0, 1917635, 648619, 30831),
    (137465860, 46928908, 844271381, 137221131, 829167629, 47351851, 14691174, 44173110, 561035847, 101721895, 110182199, 100663343, 40968, 0, 0, 0, 2839492, 1567341, 33017),
    (416977604, 708294275, 283120780, 247502466, 640155950, 605847558, 146029606, 571649327, 9480394, 108076040, 303145, 0, 0, 0, 0, 0, 15487956, 1832450, 35194),
    (138515461, 828389126, 845320237, 137376566, 830282766, 48401452, 15740775, 112331639, 67143727, 1343498, 34646088, 43000936, 0, 0, 0, 0, 3957973, 195454, 38938),
    (418027205, 872856196, 148734628, 674511878, 181928998, 907578735, 9580551, 276864514, 312051948, 377531531, 43018, 0, 0, 0, 0, 0, 14025957, 2912575, 43193),
    (14784518, 830217349, 846369902, 15742775, 47448196, 369147044, 137437196, 109052972, 78939171, 2139209, 10520683, 42, 0, 0, 0, 0, 5076454, 1281039, 41657),
    (711787142, 676740960, 710328065, 278018913, 539627527, 277067815, 310748708, 540838029, 379827210, 46763148, 11307, 0, 0, 0, 0, 0, 7429894, 13797710, 48186),
    (140614663, 116654095, 75792550, 269620238, 173062184, 9516321, 138454018, 77631597, 3508236, 36808748, 44043, 0, 0, 0, 0, 0, 15206135, 2414869, 45996),
    (837457, 824214167, 1886903, 77223969, 556802050, 858791606, 693215273, 108038154, 44618758, 591477798, 49827843, 36711429, 4232270, 112244772, 46248973, 12, 7506192, 4538218, 52670),
    (9217865, 816055400, 303432335, 916882095, 304417422, 786967687, 752659623, 584060038, 241471020, 38934092, 4132, 0, 0, 0, 0, 0, 10547593, 4044770, 17862),
    (824214593, 2761522, 36347913, 892338281, 859462688, 44043274, 8052308, 37378868, 40898571, 104902198, 40391750, 38813237, 46251020, 48314373, 13357, 0, 10523265, 16141171, 56924),
    (403809289, 849839882, 304226562, 918367400, 134754959, 235584771, 753176364, 585109639, 550801639, 39983725, 5157, 0, 0, 0, 0, 0, 12069401, 8272911, 22228),
    (714083017, 825230434, 11324449, 44043912, 104506132, 926941188, 695217184, 112235029, 860886028, 46145079, 594106405, 39859303, 15840262, 14727215, 0, 0, 3711273, 7719744, 61398),
    (210806794, 438543746, 168953611, 272380779, 176992392, 687149411, 134517261, 168410925, 552122437, 41098533, 6182, 0, 0, 0, 0, 0, 13308570, 1037368, 26462),
    (3844810, 104616585, 2937513, 827327586, 34614276, 38590088, 5873707, 79730198, 114087936, 561001504, 114333702, 40909367, 15775815, 47, 0, 0, 4270394, 6342027, 65149),
    (211856395, 473706666, 507293833, 177475714, 135498509, 919766308, 274217096, 308066408, 134224463, 375423535, 39943, 0, 0, 0, 0, 0, 2702507, 6196500, 30223),
    (716247691, 682447908, 6083587, 38899370, 680538902, 929083394, 103326726, 1596454, 863024141, 7354401, 108569096, 100728878, 48143, 0, 0, 0, 12925515, 8508969, 61671),
    (145862668, 180106628, 145601956, 178526030, 308131971, 552832137, 43124998, 308448047, 7374017, 106568, 33063, 0, 0, 0, 0, 0, 15389884, 6486325, 1921),
    (717297292, 682727190, 6296374, 830123044, 3224614, 48029322, 7907848, 847289443, 69739534, 566318, 1148943, 34651168, 0, 0, 0, 0, 14070876, 10389306, 7938),
    (146912269, 180754190, 146249518, 341971727, 172801195, 8595814, 137632810, 309339432, 43124963, 1048674, 295009, 0, 0, 0, 0, 0, 16473805, 3639908, 297),
    (829495949, 863083181, 813700748, 717263879, 82616359, 116009988, 38282240, 649102121, 547425295, 36813825, 2197034, 34, 0, 0, 0, 0, 8897901, 16451918, 8611),
    (821147662, 854988941, 147298477, 343020808, 173318316, 212870503, 45393028, 335712257, 302000417, 103852227, 2082, 0, 0, 0, 0, 0, 9203198, 1358197, 9120),
    (75119368, 108706600, 814750349, 40674304, 15827629, 683677194, 38845505, 849380908, 548409410, 649168996, 35843, 0, 0, 0, 0, 0, 14063592, 10601968, 15140),
    (276937743, 310779022, 345414830, 311629965, 174306561, 147062794, 369235233, 312644716, 11831362, 37949483, 3107, 0, 0, 0, 0, 0, 14253711, 10862614, 13490),
)


def split(x):
    high = x.astype(BF16)
    return high, (x - high.astype(F32)).astype(BF16)


def across_lanes(both, blocks):
    return [
        both[:, 2 * n * TOK : (2 * n + 1) * TOK] + both[:, (2 * n + 1) * TOK : 2 * (n + 1) * TOK]
        for n in range(blocks)
    ]


def attend(kv, slots, masks, first, q_ref, acc, top, total):
    keys, values = [], []
    for slot in slots:
        k_high, k_low = split(kv[slot, 0:TOK, :])
        keys += [jnp.concatenate([k_high, k_high], axis=1), jnp.concatenate([k_low, k_low], axis=1)]
        values.append(jnp.concatenate(split(kv[slot, KEY_ROWS:ROWS, :]), axis=1))
    keys, values = jnp.concatenate(keys, axis=0), jnp.concatenate(values, axis=0)
    both = lax.dot_general(
        q_ref[...], keys, (((1,), (1,)), ((), ())), preferred_element_type=F32
    )
    scores = [
        jnp.where(jnp.concatenate([mask] * HEADS, axis=0), score, MASKED)
        for mask, score in zip(masks, across_lanes(both, len(slots)))
    ]
    high = functools.reduce(jnp.maximum, scores)
    high = jnp.broadcast_to(jnp.max(high, axis=1, keepdims=True), high.shape)
    if not first:
        old = top[...]
        high = jnp.maximum(old, high)
        factor = jnp.exp2(old - high)
    top[...] = high
    weights = [jnp.exp2(score - high) for score in scores]
    added = functools.reduce(jnp.add, weights)
    w_high, w_low = zip(*[split(weight) for weight in weights])
    both = jnp.dot(jnp.concatenate(w_high, axis=1), values, preferred_element_type=F32)
    rest = jnp.dot(jnp.concatenate(w_low, axis=1), values[:, :TOK], preferred_element_type=F32)
    mixed = across_lanes(both, 1)[0] + rest
    total[...] = added if first else total[...] * factor + added
    acc[...] = mixed if first else acc[...] * factor + mixed


def kernel(
    planes, queries, keys, values, segment, out, kv, seg_raw, q_raw, q_ref, acc, top, total,
    load_sem, send_sem, recv_sem,
):
    inner, outer = lax.axis_index("inner"), lax.axis_index("outer")
    x, z = lax.div(inner, RING), lax.rem(inner, RING)
    plane, core = lax.div(outer, 2), lax.rem(outer, 2)
    up, down, across = lax.rem(z + 1, RING), lax.rem(z + RING - 1, RING), 1 - x
    ahead, behind = lax.rem(plane + 1, planes), lax.rem(plane + planes - 1, planes)
    far = planes // 2

    def at(to_plane, to_x, to_z, to_core):
        return {"inner": to_x * RING + to_z, "outer": to_plane * 2 + to_core}

    loads = [
        pltpu.make_async_copy(segment, seg_raw, load_sem.at[0]),
        pltpu.make_async_copy(keys, kv.at[OWN, pl.ds(0, TOK)], load_sem.at[1]),
        pltpu.make_async_copy(values, kv.at[OWN, pl.ds(KEY_ROWS, TOK)], load_sem.at[2]),
        pltpu.make_async_copy(queries, q_raw, load_sem.at[3]),
    ]
    for load in loads:
        load.start()

    barrier = pltpu.get_barrier_semaphore()

    def greet(device):
        pl.semaphore_signal(barrier, inc=1, device_id=device, device_id_type=MESH)

    for to_x, to_z in ((x, up), (x, down), (across, z)):
        for to_core in (0, 1):
            greet(at(plane, to_x, to_z, to_core))
    greet(at(plane, x, z, 1 - core))

    @pl.when(core == 0)
    def _():
        greet(at(behind, x, z, 0))
        greet(at(behind, x, z, 1))

    @pl.when((core == 0) & (x == 0))
    def _():
        greet(at(behind, 1, z, 1))

    def lookup(options, n, each, width):
        word, rest = lax.div(n, each), lax.rem(n, each)
        packed = options[0]
        for k in range(1, len(options)):
            packed = jnp.where(word == k, options[k], packed)
        field = lax.rem(packed, 1 << width)
        for k in range(1, each):
            field = jnp.where(
                rest == k, lax.rem(lax.div(packed, 1 << (width * k)), 1 << width), field
            )
        return field

    def event_of(n):
        return lookup(words[:16], n, 3, 10)

    def slot_of(n):
        return lookup(words[16:], n, 6, 4)

    def bit(event, place):
        return lax.rem(lax.div(event, 1 << place), 2) == 1

    def piece(held, slot, part, device, way):
        first, count = PARTS[part]
        here = keys if held is OWN and part == 0 else kv.at[held, pl.ds(first, count)]
        return pltpu.make_async_remote_copy(
            src_ref=here,
            dst_ref=kv.at[slot, pl.ds(first, count)],
            send_sem=send_sem.at[way, held, part],
            recv_sem=recv_sem.at[slot, part],
            device_id=device,
            device_id_type=MESH,
        )


    def absent(slot):
        kept = (lax.div(slot, RING) == x) & (lax.rem(slot, RING) < z)
        same = lax.div(slot, RING) == x
        return (plane == 0) & (core == 0) & (slot < PASSING) & ~kept & (same | (x == 0))

    def straight(to_x, hops):
        low = jnp.where(to_x == 0, 4, 2)
        return (hops >= low) & (hops <= low + 2)

    def direct(index):
        return (plane != planes - 1) & ((plane != far - 1) | straight(x, index - z))

    def onward(event, part, act):
        held = lax.rem(event, 32)
        index, passing = lax.rem(held, RING), held >= PASSING
        crossed = (held < PASSING) & (lax.div(held, RING) != x)
        is_o = passing | (~crossed & (core == 1) & (index < z))
        here = x * RING + index
        there = ~absent(held)
        for way, to_z in ((0, up), (1, down)):
            below = index < to_z
            to_core = jnp.where(below, jnp.where(is_o, 1, 0), jnp.where(is_o, across, 1))
            to_core = jnp.where(crossed, core, to_core)
            to_slot = jnp.where(is_o, jnp.where(below, here, PASSING + index), held)

            @pl.when(bit(event, 7 + way) & there)
            def _():
                act(piece(held, to_slot, part, at(plane, x, to_z, to_core), way))

        @pl.when(bit(event, 9) & ~(is_o & ~direct(index)))
        def _():
            aside = {
                "inner": jnp.where(is_o, inner, across * RING + z),
                "outer": jnp.where(is_o, ahead * 2, plane * 2 + x),
            }
            act(piece(held, here, part, aside, 2))

        from_near = (plane == far - 1) & (x == 1) & (core == 1)
        from_far = (plane == far) & (x == 0) & (core == 0)
        to_x = jnp.where(from_near, 0, 1)

        @pl.when(crossed & (index >= z) & (from_near | from_far) & ~straight(to_x, index - z))
        def _():
            act(piece(held, held, part, at(far, to_x, z, 0), 2))

    def own_onward(part, act):
        for way, to_z in ((0, up), (1, down)):
            hops = lax.rem(to_z - z + RING, RING)
            below = z < to_z
            to_core = jnp.where(below, core, jnp.where(core == 1, across, 1))
            to_slot = jnp.where((core == 1) & ~below, PASSING + z, inner)
            act(piece(OWN, to_slot, part, at(plane, x, to_z, to_core), way))

        @pl.when(core == 0)
        def _():
            act(piece(OWN, inner, part, at(plane, across, z, x), 2))
            act(piece(OWN, inner, part, at(plane, x, z, 1), 3))

        @pl.when((core == 1) & direct(z))
        def _():
            act(piece(OWN, inner, part, at(ahead, x, z, 0), 3))

        @pl.when((core == 1) & ((x == 0) | (plane != planes - 1)))
        def _():
            crossing = {
                "inner": across * RING + z,
                "outer": jnp.where(x == 0, plane * 2 + 1, ahead * 2),
            }
            act(piece(OWN, inner, part, crossing, 2))

    def start(copy):
        copy.start()

    def finish(copy):
        copy.wait_send()

    pl.semaphore_wait(barrier, 8 + core * x)
    own_onward(0, start)

    place = inner * 2 + core + jnp.where(plane == far, 2 * SLOTS, 0)
    words = [jnp.int32(0)] * 19
    for row, packed in enumerate(PLAN):
        words = [jnp.where(place == row, jnp.int32(p), w) for p, w in zip(packed, words)]

    loads[0].wait()
    own_seg = seg_raw[...].astype(F32)
    kv[OWN, TOK:KEY_ROWS, :] = jnp.broadcast_to(own_seg, (8, TOK))
    loads[2].wait()
    own_onward(1, start)
    loads[1].wait()

    lead = own_seg[:, 0:1]
    pieces = 2 * (SLOTS + jnp.where(core == across, RING - 1 - z, 0))

    row = lax.broadcasted_iota(jnp.int32, (TOK, TOK), 0)
    col = lax.broadcasted_iota(jnp.int32, (TOK, TOK), 1)
    seg_row = jnp.broadcast_to(own_seg, (TOK, TOK))
    seg_col = seg_row.T

    def alone():
        scale = math.log2(math.e) / math.sqrt(TOK)
        for head in range(HEADS):
            rows = slice(head * TOK, (head + 1) * TOK)
            q_high, q_low = split(q_raw[:, rows] * scale)
            q_ref[rows, 0:TOK] = q_high
            q_ref[rows, TOK : 2 * TOK] = q_low

        attend(kv, [OWN], [(seg_col == seg_row) & (col <= row)], True, q_ref, acc, top, total)

    def pair(n):
        slots = [slot_of(2 * n), slot_of(2 * n + 1)]
        masks = []
        for slot in slots:
            seg = kv[slot, TOK : TOK + 1, :]
            shared = jnp.sum(jnp.where(seg == lead, 1.0, 0.0), axis=1, keepdims=True)
            masks.append((seg_col == lead) & (col.astype(F32) >= TOK - shared))
        attend(kv, slots, masks, False, q_ref, acc, top, total)

    def each_part(event, do):
        for part in (0, 1):

            @pl.when(bit(event, 5) == (part == 1))
            def _():
                do(part)

    def turn(done):
        @pl.when(done == 0)
        def _():
            alone()

        @pl.when(done > 0)
        def _():
            pair(done - 1)

    def step(n, done):
        event = event_of(n)

        def receive(part):
            slot = lax.rem(event, 32)
            first, count = PARTS[part]

            @pl.when(absent(slot))
            def _():
                kv[slot, first : first + count, :] = jnp.zeros((count, TOK), F32)
                if part == 1:
                    kv[slot, TOK:KEY_ROWS, :] = jnp.full((8, TOK), -1.0, F32)

            @pl.when(~absent(slot))
            def _():
                piece(slot, slot, part, at(plane, x, up, core), 0).wait_recv()
                onward(event, part, start)

        each_part(event, receive)
        now = bit(event, 6)

        @pl.when(now)
        def _():
            turn(done)

        @pl.when(n >= LAG)
        def _():
            drain(n - LAG, 0)

        return done + jnp.where(now, 1, 0)

    def drain(n, carry):
        event = event_of(n)

        crosses = (plane == far - 1) | (plane == far)

        @pl.when((event >= 1 << 7) | crosses)
        def _():
            each_part(event, lambda part: onward(event, part, finish))

        return carry

    loads[3].wait()
    done = lax.fori_loop(0, pieces, step, jnp.int32(0))

    def rest(n, carry):
        turn(n)
        return carry

    lax.fori_loop(done, SLOTS // 2 + 1, rest, 0)

    for head in range(HEADS):
        rows = slice(head * TOK, (head + 1) * TOK)
        out[:, rows] = acc[rows, :] / jnp.sum(total[rows, :], axis=1, keepdims=True)

    lax.fori_loop(pieces - LAG, pieces, drain, 0)
    for part in (0, 1):
        own_onward(part, finish)


def body(queries, keys, values, segment):
    planes = lax.axis_size("outer") // 2
    rows = HEADS * TOK
    return pl.pallas_call(
        functools.partial(kernel, planes),
        name="gather_and_attend",
        out_shape=pltpu.VMEM(queries.shape, F32),
        in_specs=[pl.BlockSpec(memory_space=pltpu.HBM)] * 4,
        out_specs=pl.BlockSpec(memory_space=pltpu.VMEM),
        scratch_shapes=[
            pltpu.VMEM((OWN + 1, ROWS, TOK), F32),
            pltpu.VMEM((1, TOK), jnp.int32),
            pltpu.VMEM((TOK, rows), F32),
            pltpu.VMEM((rows, 2 * TOK), BF16),
            pltpu.VMEM((rows, TOK), F32),
            pltpu.VMEM((rows, TOK), F32),
            pltpu.VMEM((rows, TOK), F32),
            pltpu.SemaphoreType.DMA((4,)),
            pltpu.SemaphoreType.DMA((4, OWN + 1, 2)),
            pltpu.SemaphoreType.DMA((OWN, 2)),
        ],
        compiler_params=pltpu.CompilerParams(
            collective_id=0, has_side_effects=True, vmem_limit_bytes=60 << 20
        ),
    )(queries, keys, values, segment.reshape(1, TOK))


def solution(mesh):
    return jax.shard_map(
        body,
        mesh=mesh,
        in_specs=(
            P(("outer", "inner"), None),
            P(("outer", "inner"), None),
            P(("outer", "inner"), None),
            P(("outer", "inner")),
        ),
        out_specs=P(("outer", "inner"), None),
        check_vma=False,
    )
```
